128 devices in a mesh: occ: 16 (over x, z), vir: 8 (over y, core).
Axes of the slice: x: 4, y: 4, z: 4, core: 2. Of those that a mesh axis runs over, the one named last changes fastest.
Arguments:
- amplitudes: bfloat16 [512, 32768], P('occ', 'vir'), may hold values from -6 to 6
- tile_live: int32 [16, 32], P('occ', 'vir'), may hold values from 0 to 1, as said below
- integrals: bfloat16 [32, 32, 1024, 1024], P('occ', 'vir'), may hold values from -0.03125 to 0.03125
- block_live: int32 [32, 32], P('occ', 'vir'), may hold values 0 or 1
- row_owner: int32 [32], replicated, may hold values from 0 to 31, each once
Outputs:
- residual: float32 [512, 32768], P('occ', 'vir')
The draws below stay inside these ranges and needn't reach their ends.
Inputs may be any that keep to these rules, and one draw needn't show every extreme that they name: `tile_live`: in each pair block and each range of 4 tile pairs between 1 and 2 tiles are nonzero; some range has exactly 2. `row_owner`: each tile pair stands in exactly one slot.
All inputs are finite; a program needn't handle non-finite values. No bound on the sum of `block_live` on one device may be relied on, other than what follows from the above.
Results may differ from the reference program's by a relative error of at most 0.0003.
Values may be sent and summed in bfloat16 or wider, within the bound.
No kernel may reach another device: no remote copies, remote signals or barrier semaphores. Data moves between devices by JAX's collectives and lax.ppermute only.
A program may use at most 128 MiB of HBM per device.

```python
import jax
import jax.numpy as jnp
from jax import lax

W = 32
TP_DEV = 4
NP = 32
T_LIVE = 2
PAIRS = 512
N_OCC = 16
N_VIR = 8


def draw_tile_live(key, part):
    key = jax.random.fold_in(key, 11)
    count_key, force_key, order_key = jax.random.split(key, 3)
    counts = jax.random.randint(count_key, (N_OCC, N_VIR), 1, T_LIVE + 1)
    forced = jax.random.randint(force_key, (), 0, N_OCC * N_VIR)
    position = jnp.arange(N_OCC * N_VIR, dtype=jnp.int32).reshape(N_OCC, N_VIR)
    counts = jnp.where(position == forced, T_LIVE, counts)
    order_keys = jax.random.split(order_key, N_OCC * N_VIR)
    ranks = jax.vmap(lambda one_key: jax.random.permutation(one_key, TP_DEV))(order_keys)
    ranks = ranks.reshape(N_OCC, N_VIR, TP_DEV)
    live_tiles = (ranks < counts[:, :, None]).astype(jnp.int32)
    return live_tiles.reshape(N_OCC, N_VIR * TP_DEV)


def touch_ends(entries, stream_key, least, high):
    place = [jax.random.randint(jax.random.fold_in(stream_key, axis), (), 0, length) for axis, length in enumerate(entries.shape)]
    widest = entries.shape.index(max(entries.shape))
    beside = place[:widest] + [(place[widest] + 1) % entries.shape[widest]] + place[widest + 1:]
    return entries.at[tuple(place)].set(least).at[tuple(beside)].set(high)


def steps_of(stream_key, shape, shards, low, largest):
    level = 1.0
    for dim, shards_of in shards:
        heights = jax.random.uniform(jax.random.fold_in(jax.random.fold_in(stream_key, 6), dim), (shards_of,), jnp.float32, low / len(shards), largest / len(shards))
        level = level * jnp.repeat(jnp.exp(heights), shape[dim] // shards_of).reshape((-1,) + (1,) * (len(shape) - 1 - dim))
    return level


def centred(own_key, extent, deviation, reach, shards=(), kind=jnp.bfloat16):
    result = jax.random.normal(own_key, extent, jnp.float32) * deviation
    if len(shards) > 0:
        result = steps_of(own_key, extent, shards, -0.22, 0.18) * result
    return jnp.clip(result, min=-reach, max=reach).astype(kind)


def setup_inputs(seed: int = 0) -> dict:
    arg_keys = jax.random.split(jax.random.key(seed), 6)
    amplitudes = centred(arg_keys[0], (PAIRS, NP * W * W), 1.0, 6.0, ((0, 16), (1, 8)))
    tile_live = draw_tile_live(jax.random.fold_in(arg_keys[5], 71), 0)
    integrals = centred(arg_keys[2], (NP, NP, W * W, W * W), (NP * W * W) ** -0.5, 0.03125, ((0, 16), (1, 8)))
    block_live = touch_ends((jax.random.randint(arg_keys[3], (NP, NP), 0, 4) < 3).astype(jnp.int32), jax.random.fold_in(arg_keys[3], 1), 0, 1)
    row_owner = jax.random.permutation(arg_keys[4], NP).astype(jnp.int32)
    return dict(amplitudes=amplitudes, tile_live=tile_live, integrals=integrals, block_live=block_live, row_owner=row_owner)


def reference(amplitudes, tile_live, integrals, block_live, row_owner):
    pair_rows = amplitudes.shape[0]
    tile_count = tile_live.shape[1]
    entry_count = integrals.shape[2]
    range_count = tile_count // TP_DEV
    live_rows = jnp.repeat(tile_live, pair_rows // tile_live.shape[0], axis=0)
    amp_full = amplitudes.reshape(pair_rows, tile_count, entry_count).astype(jnp.float32)
    amp_full = amp_full * live_rows[:, :, None].astype(jnp.float32)
    amp_full = amp_full.reshape(pair_rows, range_count, TP_DEV, entry_count)

    def one_slot(slot_index):
        slot_blocks = integrals[slot_index].astype(jnp.float32)
        slot_blocks = slot_blocks * block_live[slot_index][:, None, None].astype(jnp.float32)
        slot_blocks = slot_blocks.reshape(range_count, TP_DEV, entry_count, entry_count)
        range_terms = jnp.einsum("pvtw,vtwx->vpx", amp_full, slot_blocks)
        return jnp.sum(range_terms, axis=0)

    slot_sums = lax.map(one_slot, jnp.arange(tile_count, dtype=jnp.int32))
    placed = jnp.zeros_like(slot_sums).at[row_owner].set(slot_sums)
    return jnp.transpose(placed, (1, 0, 2)).reshape(pair_rows, tile_count * entry_count)
```

```python
import functools

import jax
import jax.numpy as jnp
from jax import lax
from jax.experimental import pallas as pl
from jax.experimental.pallas import tpu as pltpu
from jax.sharding import PartitionSpec as P

RING = 4
TILES = 4
LIVE = 2
ROWS = 32
ENTRY = 1024
SLOTS = 2
BLOCKS = 16
LANES = 128
KB = ENTRY // LANES
PIECE = KB // 2 * LIVE * ROWS
META = 16
HALF = ENTRY // 2
CHUNK = 256
CODE = 32700.0
TINY = 1e-33

f32, bf16, i32, i16 = jnp.float32, jnp.bfloat16, jnp.int32, jnp.int16
VMEM = pl.BlockSpec(memory_space=pltpu.VMEM)
SMEM = pl.BlockSpec(memory_space=pltpu.SMEM)
HBM = pl.BlockSpec(memory_space=pl.ANY)


def shape(dims, dtype):
    return jax.ShapeDtypeStruct(dims, dtype)


def params(mib=16):
    return pltpu.CompilerParams(vmem_limit_bytes=mib * 1024 * 1024)


def pack_kernel(live_ref, amp_ref, first_ref, second_ref):
    live = [live_ref[0, c] != 0 for c in range(TILES)]
    c0 = jnp.int32(0)
    for c in reversed(range(TILES)):
        c0 = jnp.where(live[c], c, c0)
    c1 = jnp.int32(TILES)
    for c in reversed(range(TILES)):
        c1 = jnp.where(live[c] & (c > c0), c, c1)
    for slot, c in enumerate((c0, jnp.minimum(c1, TILES - 1))):
        for kb in range(KB):
            start = pl.multiple_of(c * ENTRY + kb * LANES, LANES)
            part = amp_ref[:, pl.ds(start, LANES)]
            half, k = divmod(kb, KB // 2)
            (first_ref, second_ref)[half][pl.ds((k * LIVE + slot) * ROWS, ROWS), :] = part
    row = lax.broadcasted_iota(i32, (META, LANES), 0)
    first_ref[pl.ds(PIECE, META), :] = jnp.where(row < 8, c0, c1).astype(f32).astype(bf16)


def pack(tile_live, amplitudes):
    return pl.pallas_call(
        pack_kernel,
        out_shape=(shape((PIECE + META, LANES), bf16), shape((PIECE, LANES), bf16)),
        in_specs=[SMEM, VMEM],
        out_specs=(VMEM, VMEM),
        compiler_params=params(),
    )(tile_live, amplitudes)


def occ_shift(value, dx, dz):
    pairs = [
        (x * RING + z, (x + dx) % RING * RING + (z + dz) % RING) for x in range(RING) for z in range(RING)
    ]
    return lax.ppermute(value, "occ", pairs)


def vir_shift(value, dy, dc):
    pairs = [(y * 2 + c, (y + dy) % RING * 2 + (c + dc) % 2) for y in range(RING) for c in range(2)]
    return lax.ppermute(value, "vir", pairs)


def compute_kernel(half_ref, live_ref, ints_ref, *refs):
    firsts, seconds = refs[:RING], refs[RING : 2 * RING]
    out_ref, left, block, product, meta_f, meta_v, meta, count, where, sems, meta_sem = refs[2 * RING :]
    half = pl.multiple_of(half_ref[0] * HALF, HALF)

    def fetch(r, c):
        return pltpu.make_async_copy(
            ints_ref.at[r, c, :, pl.ds(half, HALF)], block.at[c * SLOTS + r], sems.at[c * SLOTS + r]
        )

    for c in range(TILES):
        for r in range(SLOTS):
            pl.when(live_ref[r, c] != 0)(lambda: fetch(r, c).start())

    for e in range(RING):
        for d in range(RING):
            o = e * RING + d
            tags = firsts[e][pl.ds(d * (PIECE + META) + PIECE, META), :].astype(f32)
            meta_f[pl.ds(o * META, META), :] = tags
    meta_v[...] = meta_f[...].astype(i32)
    copy = pltpu.make_async_copy(meta_v, meta, meta_sem)
    copy.start()
    out_ref[...] = jnp.zeros_like(out_ref)
    copy.wait()
    for c in range(TILES):
        count[c] = 0

    for e in range(RING):
        for d in range(RING):
            o = e * RING + d
            for slot in range(LIVE):
                c = meta[o * META + slot * 8, 0]

                @pl.when(c < TILES)
                def _():
                    at = count[c]
                    count[c] = at + 1
                    where[c * BLOCKS + at] = o
                    rows = pl.multiple_of(at * ROWS, ROWS)
                    for kb in range(KB):
                        h, k = divmod(kb, KB // 2)
                        source, base = (
                            (firsts[e], d * (PIECE + META)) if h == 0 else (seconds[d], e * PIECE)
                        )
                        left[c, pl.ds(rows, ROWS), kb * LANES : (kb + 1) * LANES] = source[
                            pl.ds(base + (k * LIVE + slot) * ROWS, ROWS), :
                        ]

    def one_block(i, carry):
        c, r = i // SLOTS, i % SLOTS

        @pl.when(live_ref[r, c] != 0)
        def _():
            fetch(r, c).wait()
            n = count[c]

            def one_chunk(j, inner):
                product[...] = jnp.dot(
                    left[c, pl.ds(pl.multiple_of(j * CHUNK, CHUNK), CHUNK), :],
                    block[i],
                    preferred_element_type=f32,
                )

                def add(t, last):
                    o = where[c * BLOCKS + j * (CHUNK // ROWS) + t]
                    rows = pl.multiple_of(t * ROWS, ROWS)
                    for q in range(RING):
                        at = pl.ds(pl.multiple_of((o * SLOTS + r) * ROWS, ROWS), ROWS)
                        out_ref[q, at, :] += product[pl.ds(rows, ROWS), q * LANES : (q + 1) * LANES]
                    return last

                lax.fori_loop(0, jnp.minimum(n - j * (CHUNK // ROWS), CHUNK // ROWS), add, 0)
                return inner

            lax.fori_loop(0, pl.cdiv(n * ROWS, CHUNK), one_chunk, 0)

        return carry

    lax.fori_loop(0, TILES * SLOTS, one_block, 0)


def compute(half, block_live, integrals, firsts, seconds):
    return pl.pallas_call(
        compute_kernel,
        out_shape=shape((RING, BLOCKS * SLOTS * ROWS, LANES), f32),
        in_specs=[SMEM, SMEM, HBM] + [VMEM] * (2 * RING),
        out_specs=VMEM,
        scratch_shapes=[
            pltpu.VMEM((TILES, BLOCKS * ROWS, ENTRY), bf16),
            pltpu.VMEM((TILES * SLOTS, ENTRY, HALF), bf16),
            pltpu.VMEM((CHUNK, HALF), f32),
            pltpu.VMEM((BLOCKS * META, LANES), f32),
            pltpu.VMEM((BLOCKS * META, LANES), i32),
            pltpu.SMEM((BLOCKS * META, LANES), i32),
            pltpu.SMEM((TILES,), i32),
            pltpu.SMEM((TILES * BLOCKS,), i32),
            pltpu.SemaphoreType.DMA((TILES * SLOTS,)),
            pltpu.SemaphoreType.DMA,
        ],
        compiler_params=params(32),
        cost_estimate=pl.CostEstimate(flops=2 * 512 * 4096 * 1024, bytes_accessed=8 << 20, transcendentals=0),
    )(half, block_live, integrals, *firsts, *seconds)


def encode(value):
    top = jnp.maximum(jnp.max(jnp.abs(value), axis=0, keepdims=True), TINY)
    exponent = jnp.ceil(jnp.log(top) * (8.0 / 0.6931471805599453) + 0.01)
    inverse = jnp.exp(exponent * (-0.6931471805599453 / 8.0)) * CODE
    return jnp.round(value * inverse).astype(i32).astype(i16), exponent


def scale_of(exponent):
    return jnp.exp(exponent * (0.6931471805599453 / 8.0)) * (1.0 / CODE)


SUMS = BLOCKS * SLOTS
SUM_ROWS = SUMS * ROWS


def core_sum_kernel(y_ref, mine_ref, other_ref, own_ref, *refs):
    sends, exps = refs[: RING - 1], refs[RING - 1]
    y = y_ref[0]
    for d in range(RING):
        q = lax.rem(y + d, RING)
        if d == 0:
            own_ref[...] = mine_ref[q] + other_ref[q]
            continue

        def group(g, carry):
            at = pl.ds(pl.multiple_of(g * ROWS, ROWS), ROWS)
            codes, exponent = encode(mine_ref[q, at, :] + other_ref[q, at, :])
            sends[d - 1][at, :] = codes
            exps[pl.ds(g, 1), :] = exponent
            return carry

        lax.fori_loop(0, SUMS, group, 0, unroll=4)
        sends[d - 1][pl.ds(SUM_ROWS, SUMS), :] = exps[...].astype(i32).astype(i16)


def core_sum(y, mine, other):
    code = shape((SUM_ROWS + SUMS, LANES), i16)
    return pl.pallas_call(
        core_sum_kernel,
        out_shape=(shape((SUM_ROWS, LANES), f32), code, code, code),
        in_specs=[SMEM, VMEM, VMEM],
        out_specs=(VMEM,) * RING,
        scratch_shapes=[pltpu.VMEM((SUMS, LANES), f32)],
        compiler_params=params(),
    )(y, mine, other)


PART = SLOTS * ROWS + META


def ring_sum_kernel(place_ref, own_ref, a_ref, b_ref, c_ref, out_ref, scales, exps):
    x, z = place_ref[0], place_ref[1]
    codes = (a_ref, b_ref, c_ref)
    for d in range(RING - 1):
        scales[d] = scale_of(codes[d][pl.ds(SUM_ROWS, SUMS), :].astype(i32).astype(f32))
    exps[...] = jnp.zeros_like(exps)

    def block(o, carry):
        e, d = o // RING, lax.rem(o, RING)
        to = lax.rem(x - e + RING, RING) * RING + lax.rem(z - d + RING, RING)
        for r in range(SLOTS):
            g = o * SLOTS + r
            at = pl.ds(pl.multiple_of(g * ROWS, ROWS), ROWS)
            total = own_ref[at, :]
            for k in range(RING - 1):
                total += codes[k][at, :].astype(i32).astype(f32) * scales[k, pl.ds(g, 1), :]
            code, exponent = encode(total)
            out_ref[to, r * ROWS : (r + 1) * ROWS, :] = code
            exps[r : r + 1, :] = exponent
        out_ref[to, SLOTS * ROWS : PART, :] = exps[...].astype(i32).astype(i16)
        return carry

    lax.fori_loop(0, BLOCKS, block, 0, unroll=2)


def ring_sum(place, own, codes):
    return pl.pallas_call(
        ring_sum_kernel,
        out_shape=shape((BLOCKS, PART, LANES), i16),
        in_specs=[SMEM] + [VMEM] * RING,
        out_specs=VMEM,
        scratch_shapes=[pltpu.VMEM((RING - 1, SUMS, LANES), f32), pltpu.VMEM((META, LANES), f32)],
        compiler_params=params(),
    )(place, own, *codes)


RANGES = 8
DEST = TILES * ROWS + META


def reorder_kernel(owner_ref, in_ref, out_ref, exps):
    for s in range(BLOCKS * SLOTS):
        owner, r = divmod(s, SLOTS)
        p = owner_ref[s]
        v, t = p // TILES, lax.rem(p, TILES)
        out_ref[v, pl.ds(pl.multiple_of(t * ROWS, ROWS), ROWS), :] = in_ref[owner, r * ROWS : (r + 1) * ROWS, :]
        tags = in_ref[owner, SLOTS * ROWS : PART, :].astype(i32).astype(f32)
        exps[pl.ds(v * META + t, 1), :] = tags[r : r + 1, :]
    for v in range(RANGES):
        out_ref[v, TILES * ROWS : DEST, :] = exps[v * META : (v + 1) * META, :].astype(i32).astype(i16)


def reorder(row_owner, parts):
    return pl.pallas_call(
        reorder_kernel,
        out_shape=shape((RANGES, DEST, LANES), i16),
        in_specs=[SMEM, VMEM],
        out_specs=VMEM,
        scratch_shapes=[pltpu.VMEM((RANGES * META, LANES), f32)],
        compiler_params=params(),
    )(row_owner, parts)


def finish_kernel(in_ref, out_ref):
    for v in range(RANGES):
        y, core = divmod(v, 2)
        scale = scale_of(in_ref[v, TILES * ROWS : DEST, :].astype(i32).astype(f32))
        for t in range(TILES):
            column = t * ENTRY + core * HALF + y * LANES
            value = in_ref[v, t * ROWS : (t + 1) * ROWS, :].astype(i32).astype(f32)
            out_ref[:, column : column + LANES] = value * scale[t : t + 1, :]


def finish(parts):
    return pl.pallas_call(
        finish_kernel,
        out_shape=shape((ROWS, TILES * ENTRY), f32),
        in_specs=[VMEM],
        out_specs=VMEM,
        compiler_params=params(),
    )(parts)


def shards(amplitudes, tile_live, integrals, block_live, row_owner):
    occ, vir = lax.axis_index("occ"), lax.axis_index("vir")
    x, z, y, core = occ // RING, occ % RING, vir // 2, vir % 2
    place = jnp.stack([x, z]).astype(i32)

    first, second = pack(tile_live, amplitudes)
    along_z = jnp.concatenate([first] + [occ_shift(first, 0, d) for d in range(1, RING)], 0)
    along_x = jnp.concatenate([second] + [occ_shift(second, e, 0) for e in range(1, RING)], 0)
    firsts = [along_z] + [occ_shift(along_z, e, 0) for e in range(1, RING)]
    seconds = [along_x] + [occ_shift(along_x, 0, d) for d in range(1, RING)]

    theirs = compute((1 - core).reshape(1).astype(i32), block_live, integrals, firsts, seconds)
    other = vir_shift(theirs, 0, 1)
    mine = compute(core.reshape(1).astype(i32), block_live, integrals, firsts, seconds)
    own, *sends = core_sum(y.reshape(1).astype(i32), mine, other)
    codes = [vir_shift(sends[d - 1], d, 0) for d in range(1, RING)]
    parts = ring_sum(place, own, codes)
    parts = lax.all_to_all(parts, "occ", split_axis=0, concat_axis=0, tiled=True)
    parts = reorder(row_owner, parts)
    parts = lax.all_to_all(parts, "vir", split_axis=0, concat_axis=0, tiled=True)
    return finish(parts)


def solution(mesh):
    return jax.shard_map(
        shards,
        mesh=mesh,
        in_specs=(
            P("occ", "vir"),
            P("occ", "vir"),
            P("occ", "vir", None, None),
            P("occ", "vir"),
            P(),
        ),
        out_specs=P("occ", "vir"),
        check_vma=False,
    )
```

```python
import functools

import jax
import jax.numpy as jnp
from jax import lax
from jax.experimental import pallas as pl
from jax.experimental.pallas import tpu as pltpu
from jax.sharding import PartitionSpec as P

RING = 4
TILES = 4
LIVE = 2
ROWS = 32
ENTRY = 1024
SLOTS = 2
BLOCKS = 16
LANES = 128
KB = ENTRY // LANES
META = 16
TAG = KB * LIVE * ROWS
PIECE = TAG + META
HALF = ENTRY // 2
CHUNK = 256
SIZES = (64, 128, CHUNK)
CODE = 32700.0
TINY = 1e-33

f32, bf16, i32, i16 = jnp.float32, jnp.bfloat16, jnp.int32, jnp.int16
VMEM = pl.BlockSpec(memory_space=pltpu.VMEM)
SMEM = pl.BlockSpec(memory_space=pltpu.SMEM)
HBM = pl.BlockSpec(memory_space=pltpu.HBM)
ANY = pl.BlockSpec(memory_space=pl.ANY)


def shape(dims, dtype):
    return jax.ShapeDtypeStruct(dims, dtype)


def in_hbm(*arrays):
    return [pltpu.with_memory_space_constraint(a, pltpu.HBM) for a in arrays]


def in_vmem(*arrays):
    return [pltpu.with_memory_space_constraint(a, pltpu.VMEM) for a in arrays]


def params(mib=4):
    return pltpu.CompilerParams(vmem_limit_bytes=mib * 1024 * 1024)


def pack_kernel(live_hbm, amp_hbm, out_ref, amp, live, sems):
    copies = (
        pltpu.make_async_copy(live_hbm, live, sems.at[0]),
        pltpu.make_async_copy(amp_hbm, amp, sems.at[1]),
    )
    for copy in copies:
        copy.start()
    for copy in copies:
        copy.wait()
    c0 = jnp.int32(0)
    for c in reversed(range(TILES)):
        c0 = jnp.where(live[0, c] != 0, c, c0)
    c1 = jnp.int32(TILES)
    for c in reversed(range(TILES)):
        c1 = jnp.where((live[0, c] != 0) & (c > c0), c, c1)
    for slot, c in enumerate((c0, jnp.minimum(c1, TILES - 1))):
        for kb in range(KB):
            start = pl.multiple_of(c * ENTRY + kb * LANES, LANES)
            out_ref[pl.ds((kb * LIVE + slot) * ROWS, ROWS), :] = amp[:, pl.ds(start, LANES)]
    tag = jnp.full((META, LANES), c0 * 8 + c1, i32)
    out_ref[pl.ds(TAG, META), :] = tag.astype(f32).astype(bf16)


def pack(tile_live, amplitudes):
    return pl.pallas_call(
        pack_kernel,
        out_shape=shape((PIECE, LANES), bf16),
        in_specs=[HBM, HBM],
        out_specs=VMEM,
        scratch_shapes=[
            pltpu.VMEM(amplitudes.shape, bf16),
            pltpu.SMEM(tile_live.shape, i32),
            pltpu.SemaphoreType.DMA((2,)),
        ],
        compiler_params=params(),
    )(*in_hbm(tile_live, amplitudes))


def shift(value, place):
    def index(x, z, y, core):
        return ((x % RING) * RING + z % RING) * 2 * RING + (y % RING) * 2 + core % 2

    spots = [(x, z, y, c) for x in range(RING) for z in range(RING) for y in range(RING) for c in range(2)]
    return lax.ppermute(value, ("occ", "vir"), [(index(*s), index(*place(*s))) for s in spots])


def shift_first(value, n):
    return shift(value, lambda x, z, y, c: (x, z + n, y, c) if c == 0 else (x + n, z, y, c))


def shift_second(value, n):
    return shift(value, lambda x, z, y, c: (x + n, z, y, c) if c == 0 else (x, z + n, y, c))


def shift_y(value, n):
    return shift(value, lambda x, z, y, c: (x, z, y + n, c))


def shift_core(value):
    return shift(value, lambda x, z, y, c: (x, z, y, c + 1))


NEAR = (0, 1, 3)
GROUPS = (
    [(e, d) for e in NEAR for d in NEAR],
    [(2, d) for d in range(RING)] + [(e, 2) for e in NEAR],
)


def compute_kernel(group, shifts, fetches, core_ref, live_hbm, ints_hbm, block_in, *refs):
    amps = dict(zip(shifts, refs[: len(shifts)]))
    refs = refs[len(shifts) :]
    theirs_ref, mine_ref, block_ref, left, product, table_v, table, live, count, where, sem, sems = refs
    del block_in
    core = core_ref[0]
    copy_live = pltpu.make_async_copy(live_hbm, live, sem.at[0])
    copy_live.start()

    lane = lax.broadcasted_iota(i32, (8, LANES), 1)
    entries = jnp.zeros((8, LANES), i32)
    for k, (a, b) in enumerate(group):
        tag = amps[a][pl.ds(b * PIECE + TAG, META), :].astype(f32)[:8].astype(i32)
        entries = jnp.where(lane == k, tag, entries)
    table_v[...] = entries
    copy_table = pltpu.make_async_copy(table_v, table, sem.at[1])
    copy_table.start()

    def fetch(i):
        return pltpu.make_async_copy(ints_hbm.at[lax.rem(i, SLOTS), i // SLOTS], block_ref.at[i], sems.at[i])

    copy_live.wait()
    if fetches:
        for i in range(TILES * SLOTS):
            pl.when(live[i % SLOTS, i // SLOTS] != 0)(functools.partial(lambda i: fetch(i).start(), i))
    theirs_ref[...] = jnp.zeros_like(theirs_ref)
    mine_ref[...] = jnp.zeros_like(mine_ref)
    for c in range(TILES):
        count[c] = 0
    copy_table.wait()

    for k, (a, b) in enumerate(group):
        tag = table[0, k]
        o = jnp.where(core == 0, k, group.index((b, a)))
        for slot in range(LIVE):
            c = tag // 8 if slot == 0 else lax.rem(tag, 8)

            @pl.when(c < TILES)
            def _():
                at = count[c]
                count[c] = at + 1
                where[c * BLOCKS + at] = o
                rows = pl.multiple_of(at * ROWS, ROWS)
                for kb in range(KB):
                    left[c, pl.ds(rows, ROWS), kb * LANES : (kb + 1) * LANES] = amps[a][
                        pl.ds(b * PIECE + (kb * LIVE + slot) * ROWS, ROWS), :
                    ]

    def one_block(i, carry):
        c, r = i // SLOTS, lax.rem(i, SLOTS)

        @pl.when(live[r, c] != 0)
        def _():
            if fetches:
                fetch(i).wait()
            n = count[c]

            def one_chunk(j, inner):
                rest = n - j * (CHUNK // ROWS)
                start = pl.multiple_of(j * CHUNK, CHUNK)

                def multiply(rows):
                    product[:rows, :] = jnp.dot(
                        left[c, pl.ds(start, rows), :], block_ref[i], preferred_element_type=f32
                    )

                low = 0
                for rows in SIZES:
                    tiles = rows // ROWS
                    pl.when((rest > low) & ((rest <= tiles) | (rows == CHUNK)))(functools.partial(multiply, rows))
                    low = tiles

                def add(t, last):
                    o = where[c * BLOCKS + j * (CHUNK // ROWS) + t]
                    rows = pl.ds(pl.multiple_of(t * ROWS, ROWS), ROWS)
                    at = pl.ds(pl.multiple_of((o * SLOTS + r) * ROWS, ROWS), ROWS)
                    for part, ref in enumerate((mine_ref, theirs_ref)):
                        start = pl.multiple_of(jnp.where(core == 0, part, 1 - part) * HALF, HALF)
                        for q in range(RING):
                            ref[q, at, :] += product[rows, pl.ds(start + q * LANES, LANES)]
                    return last

                lax.fori_loop(0, jnp.minimum(rest, CHUNK // ROWS), add, 0)
                return inner

            lax.fori_loop(0, pl.cdiv(n * ROWS, CHUNK), one_chunk, 0)

        return carry

    lax.fori_loop(0, TILES * SLOTS, one_block, 0)


def compute(which, core, block_live, integrals, blocks, amps):
    group = GROUPS[which]
    shifts = sorted(amps)
    fetches = blocks is None
    total = pltpu.VMEM((RING, len(group) * SLOTS * ROWS, LANES), f32)
    held = (TILES * SLOTS, ENTRY, ENTRY)
    return pl.pallas_call(
        functools.partial(compute_kernel, group, shifts, fetches),
        out_shape=(total, total, pltpu.VMEM(held, bf16)),
        in_specs=[SMEM, HBM, HBM] + [SMEM if fetches else VMEM] + [VMEM] * len(shifts),
        out_specs=(VMEM,) * 3,
        input_output_aliases={} if fetches else {3: 2},
        scratch_shapes=[
            pltpu.VMEM((TILES, 2 * CHUNK, ENTRY), bf16),
            pltpu.VMEM((CHUNK, ENTRY), f32),
            pltpu.VMEM((8, LANES), i32),
            pltpu.SMEM((8, LANES), i32),
            pltpu.SMEM(block_live.shape, i32),
            pltpu.SMEM((TILES,), i32),
            pltpu.SMEM((TILES * BLOCKS,), i32),
            pltpu.SemaphoreType.DMA((2,)),
            pltpu.SemaphoreType.DMA((TILES * SLOTS,)),
        ],
        compiler_params=params(8),
        cost_estimate=pl.CostEstimate(flops=1 << 32, bytes_accessed=8 << 20, transcendentals=0),
    )(core, *in_hbm(block_live, integrals), *([core] if fetches else in_vmem(blocks)), *[amps[a] for a in shifts])


def encode(value):
    top = jnp.maximum(jnp.max(jnp.abs(value), axis=0, keepdims=True), TINY)
    exponent = jnp.ceil(jnp.log(top) * (8.0 / 0.6931471805599453) + 0.01)
    inverse = jnp.exp(exponent * (-0.6931471805599453 / 8.0)) * CODE
    return jnp.round(value * inverse).astype(i32).astype(i16), exponent


def scale_of(exponent):
    return jnp.exp(exponent * (0.6931471805599453 / 8.0)) * (1.0 / CODE)


def tag_rows(sums):
    return pl.cdiv(sums, META) * META


def core_sum_kernel(y_ref, mine_ref, other_ref, own_ref, *refs):
    sends, exps = refs[: RING - 1], refs[RING - 1]
    y = y_ref[0]
    rows = own_ref.shape[0]
    own_ref[...] = mine_ref[y] + other_ref[y]
    exps[...] = jnp.zeros_like(exps)
    for d in range(1, RING):
        q = lax.rem(y + d, RING)

        def group(g, carry):
            at = pl.ds(pl.multiple_of(g * ROWS, ROWS), ROWS)
            codes, exponent = encode(mine_ref[q, at, :] + other_ref[q, at, :])
            sends[d - 1][at, :] = codes
            exps[pl.ds(g, 1), :] = exponent
            return carry

        lax.fori_loop(0, rows // ROWS, group, 0, unroll=2)
        sends[d - 1][pl.ds(rows, exps.shape[0]), :] = exps[...].astype(i32).astype(i16)


def core_sum(y, mine, other):
    rows = mine.shape[1]
    tags = tag_rows(rows // ROWS)
    code = shape((rows + tags, LANES), i16)
    return pl.pallas_call(
        core_sum_kernel,
        out_shape=(shape((rows, LANES), f32), code, code, code),
        in_specs=[SMEM, VMEM, VMEM],
        out_specs=(VMEM,) * RING,
        scratch_shapes=[pltpu.VMEM((tags, LANES), f32)],
        compiler_params=params(),
    )(y, mine, other)


PART = SLOTS * ROWS + META


def ring_sum_kernel(group, place_ref, own_ref, a_ref, b_ref, c_ref, *refs):
    out_ref, scales, exps = refs[-3:]
    x, z = place_ref[0], place_ref[1]
    codes = (a_ref, b_ref, c_ref)
    rows, tags = own_ref.shape[0], scales.shape[1]
    for k in range(RING - 1):
        scales[k] = scale_of(codes[k][pl.ds(rows, tags), :].astype(i32).astype(f32))
    exps[...] = jnp.zeros_like(exps)
    for o, (e, d) in enumerate(group):
        to = lax.rem(x - e + RING, RING) * RING + lax.rem(z - d + RING, RING)
        for r in range(SLOTS):
            g = o * SLOTS + r
            at = pl.ds(g * ROWS, ROWS)
            total = own_ref[at, :]
            for k in range(RING - 1):
                total += codes[k][at, :].astype(i32).astype(f32) * scales[k, g : g + 1, :]
            code, exponent = encode(total)
            out_ref[to, r * ROWS : (r + 1) * ROWS, :] = code
            exps[r : r + 1, :] = exponent
        out_ref[to, SLOTS * ROWS : PART, :] = exps[...].astype(i32).astype(i16)


def ring_sum(which, place, own, codes, parts=None):
    more = [] if parts is None else [parts]
    return pl.pallas_call(
        functools.partial(ring_sum_kernel, GROUPS[which]),
        out_shape=shape((BLOCKS, PART, LANES), i16),
        in_specs=[SMEM] + [VMEM] * (RING + len(more)),
        out_specs=VMEM,
        input_output_aliases={RING + 1: 0} if more else {},
        scratch_shapes=[
            pltpu.VMEM((RING - 1, tag_rows(own.shape[0] // ROWS), LANES), f32),
            pltpu.VMEM((META, LANES), f32),
        ],
        compiler_params=params(),
    )(place, own, *codes, *more)


RANGES = 8
DEST = TILES * ROWS + META


def reorder_kernel(owner_ref, in_ref, out_ref, exps):
    for s in range(BLOCKS * SLOTS):
        owner, r = divmod(s, SLOTS)
        p = owner_ref[s]
        v, t = p // TILES, lax.rem(p, TILES)
        out_ref[v, pl.ds(pl.multiple_of(t * ROWS, ROWS), ROWS), :] = in_ref[owner, r * ROWS : (r + 1) * ROWS, :]
        tags = in_ref[owner, SLOTS * ROWS : PART, :].astype(i32).astype(f32)
        exps[pl.ds(v * META + t, 1), :] = tags[r : r + 1, :]
    for v in range(RANGES):
        out_ref[v, TILES * ROWS : DEST, :] = exps[v * META : (v + 1) * META, :].astype(i32).astype(i16)


def reorder(row_owner, parts):
    return pl.pallas_call(
        reorder_kernel,
        out_shape=shape((RANGES, DEST, LANES), i16),
        in_specs=[SMEM, VMEM],
        out_specs=VMEM,
        scratch_shapes=[pltpu.VMEM((RANGES * META, LANES), f32)],
        compiler_params=params(),
    )(row_owner, parts)


def finish_kernel(in_ref, out_ref):
    for v in range(RANGES):
        y, core = divmod(v, 2)
        scale = scale_of(in_ref[v, TILES * ROWS : DEST, :].astype(i32).astype(f32))
        for t in range(TILES):
            column = t * ENTRY + core * HALF + y * LANES
            value = in_ref[v, t * ROWS : (t + 1) * ROWS, :].astype(i32).astype(f32)
            out_ref[:, column : column + LANES] = value * scale[t : t + 1, :]


def finish(parts):
    return pl.pallas_call(
        finish_kernel,
        out_shape=shape((ROWS, TILES * ENTRY), f32),
        in_specs=[VMEM],
        out_specs=VMEM,
        compiler_params=params(),
    )(parts)


def shards(amplitudes, tile_live, integrals, block_live, row_owner):
    occ, vir = lax.axis_index("occ"), lax.axis_index("vir")
    x, z, y, core = occ // RING, occ % RING, vir // 2, vir % 2
    place = jnp.stack([x, z]).astype(i32)

    packed = pack(tile_live, amplitudes)
    row = jnp.concatenate([packed] + [shift_first(packed, b) for b in range(1, RING)], 0)
    amps = {0: row, 1: shift_second(row, 1), 3: shift_second(row, 3)}
    late, amps[3] = lax.optimization_barrier((row, amps[3]))
    amps[2] = shift_second(late, 2)

    which_core, which_y = core.reshape(1).astype(i32), y.reshape(1).astype(i32)

    theirs0, mine0, blocks = compute(
        0, which_core, block_live, integrals, None, {a: amps[a] for a in NEAR}
    )
    other0 = shift_core(theirs0)
    theirs1, mine1, _ = compute(1, which_core, block_live, integrals, blocks, amps)
    other1 = shift_core(theirs1)
    own0, *sends0 = core_sum(which_y, mine0, other0)
    codes0 = [shift_y(sends0[d - 1], d) for d in range(1, RING)]
    own1, *sends1 = core_sum(which_y, mine1, other1)
    codes1 = [shift_y(sends1[d - 1], d) for d in range(1, RING)]
    parts = ring_sum(0, place, own0, codes0)
    parts = ring_sum(1, place, own1, codes1, parts)
    parts = lax.all_to_all(parts, "occ", split_axis=0, concat_axis=0, tiled=True)
    parts = reorder(row_owner, parts)
    parts = lax.all_to_all(parts, "vir", split_axis=0, concat_axis=0, tiled=True)
    return finish(parts)


def solution(mesh):
    return jax.shard_map(
        shards,
        mesh=mesh,
        in_specs=(
            P("occ", "vir"),
            P("occ", "vir"),
            P("occ", "vir", None, None),
            P("occ", "vir"),
            P(),
        ),
        out_specs=P("occ", "vir"),
        check_vma=False,
    )
```

```python
import functools

import jax
import jax.numpy as jnp
from jax import lax
from jax.experimental import pallas as pl
from jax.experimental.pallas import tpu as pltpu
from jax.sharding import PartitionSpec as P

RING = 4
TILES = 4
LIVE = 2
ROWS = 32
ENTRY = 1024
SLOTS = 2
BLOCKS = 16
LANES = 128
KB = ENTRY // LANES
META = 16
TAG = KB * LIVE * ROWS
PIECE = TAG + META
HALF = ENTRY // 2
CHUNK = 256
SIZES = (64, 128, CHUNK)
CODE = 32700.0
TINY = 1e-33

f32, bf16, i32, i16 = jnp.float32, jnp.bfloat16, jnp.int32, jnp.int16
VMEM = pl.BlockSpec(memory_space=pltpu.VMEM)
SMEM = pl.BlockSpec(memory_space=pltpu.SMEM)
HBM = pl.BlockSpec(memory_space=pltpu.HBM)
ANY = pl.BlockSpec(memory_space=pl.ANY)


def shape(dims, dtype):
    return jax.ShapeDtypeStruct(dims, dtype)


def position():
    occ, vir = lax.axis_index("occ"), lax.axis_index("vir")
    return occ // RING, lax.rem(occ, RING), vir // 2, lax.rem(vir, 2)


def in_hbm(*arrays):
    return [pltpu.with_memory_space_constraint(a, pltpu.HBM) for a in arrays]


def in_vmem(*arrays):
    return [pltpu.with_memory_space_constraint(a, pltpu.VMEM) for a in arrays]


def params(mib=4):
    return pltpu.CompilerParams(vmem_limit_bytes=mib * 1024 * 1024)


def pack_kernel(live_hbm, amp_hbm, out_ref, amp, live, sems):
    copies = (
        pltpu.make_async_copy(live_hbm, live, sems.at[0]),
        pltpu.make_async_copy(amp_hbm, amp, sems.at[1]),
    )
    for copy in copies:
        copy.start()
    for copy in copies:
        copy.wait()
    c0 = jnp.int32(0)
    for c in reversed(range(TILES)):
        c0 = jnp.where(live[0, c] != 0, c, c0)
    c1 = jnp.int32(TILES)
    for c in reversed(range(TILES)):
        c1 = jnp.where((live[0, c] != 0) & (c > c0), c, c1)
    for slot, c in enumerate((c0, jnp.minimum(c1, TILES - 1))):
        for kb in range(KB):
            start = pl.multiple_of(c * ENTRY + kb * LANES, LANES)
            out_ref[pl.ds((kb * LIVE + slot) * ROWS, ROWS), :] = amp[:, pl.ds(start, LANES)]
    tag = jnp.full((META, LANES), c0 * 8 + c1, i32)
    out_ref[pl.ds(TAG, META), :] = tag.astype(f32).astype(bf16)


def pack(tile_live, amplitudes):
    return pl.pallas_call(
        pack_kernel,
        out_shape=shape((PIECE, LANES), bf16),
        in_specs=[HBM, HBM],
        out_specs=VMEM,
        scratch_shapes=[
            pltpu.VMEM(amplitudes.shape, bf16),
            pltpu.SMEM(tile_live.shape, i32),
            pltpu.SemaphoreType.DMA((2,)),
        ],
        compiler_params=params(),
    )(*in_hbm(tile_live, amplitudes))


def shift(value, place):
    def index(x, z, y, core):
        return ((x % RING) * RING + z % RING) * 2 * RING + (y % RING) * 2 + core % 2

    spots = [(x, z, y, c) for x in range(RING) for z in range(RING) for y in range(RING) for c in range(2)]
    return lax.ppermute(value, ("occ", "vir"), [(index(*s), index(*place(*s))) for s in spots])


def shift_first(value, n):
    return shift(value, lambda x, z, y, c: (x, z + n, y, c) if c == 0 else (x + n, z, y, c))


def shift_second(value, n):
    return shift(value, lambda x, z, y, c: (x + n, z, y, c) if c == 0 else (x, z + n, y, c))


def shift_y(value, n):
    return shift(value, lambda x, z, y, c: (x, z, y + n, c))


def shift_core(value):
    return shift(value, lambda x, z, y, c: (x, z, y, c + 1))


def fetch_kernel(live_hbm, ints_hbm, after_ref, block_ref, live, sem, sems):
    del after_ref
    copy = pltpu.make_async_copy(live_hbm, live, sem)
    copy.start()
    copy.wait()

    def fetch(r, c):
        i = c * SLOTS + r
        return pltpu.make_async_copy(ints_hbm.at[r, c], block_ref.at[i], sems.at[i])

    for c in range(TILES):
        for r in range(SLOTS):
            pl.when(live[r, c] != 0)(lambda: fetch(r, c).start())
    for c in range(TILES):
        for r in range(SLOTS):
            pl.when(live[r, c] != 0)(lambda: fetch(r, c).wait())


def fetch_blocks(block_live, integrals, after):
    return pl.pallas_call(
        fetch_kernel,
        out_shape=pltpu.VMEM((TILES * SLOTS, ENTRY, ENTRY), bf16),
        in_specs=[HBM, HBM, ANY],
        out_specs=VMEM,
        scratch_shapes=[
            pltpu.SMEM(block_live.shape, i32),
            pltpu.SemaphoreType.DMA,
            pltpu.SemaphoreType.DMA((TILES * SLOTS,)),
        ],
        compiler_params=params(2),
        cost_estimate=pl.CostEstimate(flops=0, bytes_accessed=32 << 20, transcendentals=0),
    )(*in_hbm(block_live, integrals), after)


NEAR = (0, 1, 3)
GROUPS = (
    [(e, d) for e in NEAR for d in NEAR],
    [(2, d) for d in range(RING)] + [(e, 2) for e in NEAR],
)


def compute_kernel(group, shifts, live_hbm, block_ref, *refs):
    amps = dict(zip(shifts, refs[: len(shifts)]))
    theirs_ref, mine_ref, left, product, table_v, table, live, count, where, sem = refs[len(shifts) :]
    core = position()[3]
    copy_live = pltpu.make_async_copy(live_hbm, live, sem.at[0])
    copy_live.start()

    lane = lax.broadcasted_iota(i32, (8, LANES), 1)
    entries = jnp.zeros((8, LANES), i32)
    for k, (a, b) in enumerate(group):
        tag = amps[a][pl.ds(b * PIECE + TAG, META), :].astype(f32)[:8].astype(i32)
        entries = jnp.where(lane == k, tag, entries)
    table_v[...] = entries
    copy_table = pltpu.make_async_copy(table_v, table, sem.at[1])
    copy_table.start()

    theirs_ref[...] = jnp.zeros_like(theirs_ref)
    mine_ref[...] = jnp.zeros_like(mine_ref)
    for c in range(TILES):
        count[c] = 0
    copy_live.wait()
    copy_table.wait()

    for k, (a, b) in enumerate(group):
        tag = table[0, k]
        o = jnp.where(core == 0, k, group.index((b, a)))
        for slot in range(LIVE):
            c = tag // 8 if slot == 0 else lax.rem(tag, 8)

            @pl.when(c < TILES)
            def _():
                at = count[c]
                count[c] = at + 1
                where[c * BLOCKS + at] = o
                rows = pl.multiple_of(at * ROWS, ROWS)
                for kb in range(KB):
                    left[c, pl.ds(rows, ROWS), kb * LANES : (kb + 1) * LANES] = amps[a][
                        pl.ds(b * PIECE + (kb * LIVE + slot) * ROWS, ROWS), :
                    ]

    def one_block(i, carry):
        c, r = i // SLOTS, lax.rem(i, SLOTS)

        @pl.when(live[r, c] != 0)
        def _():
            n = count[c]

            def one_chunk(j, inner):
                rest = n - j * (CHUNK // ROWS)
                start = pl.multiple_of(j * CHUNK, CHUNK)

                def multiply(rows):
                    product[:rows, :] = jnp.dot(
                        left[c, pl.ds(start, rows), :], block_ref[i], preferred_element_type=f32
                    )

                low = 0
                for rows in SIZES:
                    tiles = rows // ROWS
                    pl.when((rest > low) & ((rest <= tiles) | (rows == CHUNK)))(functools.partial(multiply, rows))
                    low = tiles

                def add(t, last):
                    o = where[c * BLOCKS + j * (CHUNK // ROWS) + t]
                    rows = pl.ds(pl.multiple_of(t * ROWS, ROWS), ROWS)
                    at = pl.ds(pl.multiple_of((o * SLOTS + r) * ROWS, ROWS), ROWS)
                    for part, ref in enumerate((mine_ref, theirs_ref)):
                        start = pl.multiple_of(jnp.where(core == 0, part, 1 - part) * HALF, HALF)
                        for q in range(RING):
                            ref[q, at, :] += product[rows, pl.ds(start + q * LANES, LANES)]
                    return last

                lax.fori_loop(0, jnp.minimum(rest, CHUNK // ROWS), add, 0)
                return inner

            lax.fori_loop(0, pl.cdiv(n * ROWS, CHUNK), one_chunk, 0)

        return carry

    lax.fori_loop(0, TILES * SLOTS, one_block, 0)


def compute(which, block_live, blocks, amps):
    group = GROUPS[which]
    shifts = sorted(amps)
    total = pltpu.VMEM((RING, len(group) * SLOTS * ROWS, LANES), f32)
    return pl.pallas_call(
        functools.partial(compute_kernel, group, shifts),
        out_shape=(total, total),
        in_specs=[HBM] + [VMEM] * (1 + len(shifts)),
        out_specs=(VMEM,) * 2,
        scratch_shapes=[
            pltpu.VMEM((TILES, 2 * CHUNK, ENTRY), bf16),
            pltpu.VMEM((CHUNK, ENTRY), f32),
            pltpu.VMEM((8, LANES), i32),
            pltpu.SMEM((8, LANES), i32),
            pltpu.SMEM(block_live.shape, i32),
            pltpu.SMEM((TILES,), i32),
            pltpu.SMEM((TILES * BLOCKS,), i32),
            pltpu.SemaphoreType.DMA((2,)),
        ],
        compiler_params=params(8),
        cost_estimate=pl.CostEstimate(flops=1 << 32, bytes_accessed=8 << 20, transcendentals=0),
    )(*in_hbm(block_live), *in_vmem(blocks), *[amps[a] for a in shifts])


def encode(value):
    top = jnp.maximum(jnp.max(jnp.abs(value), axis=0, keepdims=True), TINY)
    exponent = jnp.ceil(jnp.log(top) * (8.0 / 0.6931471805599453) + 0.01)
    inverse = jnp.exp(exponent * (-0.6931471805599453 / 8.0)) * CODE
    return jnp.round(value * inverse).astype(i32).astype(i16), exponent


def scale_of(exponent):
    return jnp.exp(exponent * (0.6931471805599453 / 8.0)) * (1.0 / CODE)


def tag_rows(sums):
    return pl.cdiv(sums, META) * META


def core_sum_kernel(mine_ref, other_ref, own_ref, *refs):
    sends, exps = refs[: RING - 1], refs[RING - 1]
    y = position()[2]
    rows = own_ref.shape[0]
    own_ref[...] = mine_ref[y] + other_ref[y]
    exps[...] = jnp.zeros_like(exps)
    for d in range(1, RING):
        q = lax.rem(y + d, RING)

        def group(g, carry):
            at = pl.ds(pl.multiple_of(g * ROWS, ROWS), ROWS)
            codes, exponent = encode(mine_ref[q, at, :] + other_ref[q, at, :])
            sends[d - 1][at, :] = codes
            exps[pl.ds(g, 1), :] = exponent
            return carry

        lax.fori_loop(0, rows // ROWS, group, 0, unroll=2)
        sends[d - 1][pl.ds(rows, exps.shape[0]), :] = exps[...].astype(i32).astype(i16)


def core_sum(mine, other):
    rows = mine.shape[1]
    tags = tag_rows(rows // ROWS)
    code = shape((rows + tags, LANES), i16)
    return pl.pallas_call(
        core_sum_kernel,
        out_shape=(shape((rows, LANES), f32), code, code, code),
        in_specs=[VMEM, VMEM],
        out_specs=(VMEM,) * RING,
        scratch_shapes=[pltpu.VMEM((tags, LANES), f32)],
        compiler_params=params(),
    )(mine, other)


PART = SLOTS * ROWS + META


def ring_sum_kernel(group, own_ref, a_ref, b_ref, c_ref, *refs):
    out_ref, scales, exps = refs[-3:]
    x, z = position()[:2]
    codes = (a_ref, b_ref, c_ref)
    rows, tags = own_ref.shape[0], scales.shape[1]
    for k in range(RING - 1):
        scales[k] = scale_of(codes[k][pl.ds(rows, tags), :].astype(i32).astype(f32))
    exps[...] = jnp.zeros_like(exps)
    for o, (e, d) in enumerate(group):
        to = lax.rem(x - e + RING, RING) * RING + lax.rem(z - d + RING, RING)
        for r in range(SLOTS):
            g = o * SLOTS + r
            at = pl.ds(g * ROWS, ROWS)
            total = own_ref[at, :]
            for k in range(RING - 1):
                total += codes[k][at, :].astype(i32).astype(f32) * scales[k, g : g + 1, :]
            code, exponent = encode(total)
            out_ref[to, r * ROWS : (r + 1) * ROWS, :] = code
            exps[r : r + 1, :] = exponent
        out_ref[to, SLOTS * ROWS : PART, :] = exps[...].astype(i32).astype(i16)


def ring_sum(which, own, codes, parts=None):
    more = [] if parts is None else [parts]
    return pl.pallas_call(
        functools.partial(ring_sum_kernel, GROUPS[which]),
        out_shape=shape((BLOCKS, PART, LANES), i16),
        in_specs=[VMEM] * (RING + len(more)),
        out_specs=VMEM,
        input_output_aliases={RING: 0} if more else {},
        scratch_shapes=[
            pltpu.VMEM((RING - 1, tag_rows(own.shape[0] // ROWS), LANES), f32),
            pltpu.VMEM((META, LANES), f32),
        ],
        compiler_params=params(),
    )(own, *codes, *more)


RANGES = 8
DEST = TILES * ROWS + META


def reorder_kernel(owner_ref, in_ref, out_ref, exps):
    for s in range(BLOCKS * SLOTS):
        owner, r = divmod(s, SLOTS)
        p = owner_ref[s]
        v, t = p // TILES, lax.rem(p, TILES)
        out_ref[v, pl.ds(pl.multiple_of(t * ROWS, ROWS), ROWS), :] = in_ref[owner, r * ROWS : (r + 1) * ROWS, :]
        tags = in_ref[owner, SLOTS * ROWS : PART, :].astype(i32).astype(f32)
        exps[pl.ds(v * META + t, 1), :] = tags[r : r + 1, :]
    for v in range(RANGES):
        out_ref[v, TILES * ROWS : DEST, :] = exps[v * META : (v + 1) * META, :].astype(i32).astype(i16)


def reorder(row_owner, parts):
    return pl.pallas_call(
        reorder_kernel,
        out_shape=shape((RANGES, DEST, LANES), i16),
        in_specs=[SMEM, VMEM],
        out_specs=VMEM,
        scratch_shapes=[pltpu.VMEM((RANGES * META, LANES), f32)],
        compiler_params=params(),
    )(row_owner, parts)


def finish_kernel(in_ref, out_ref):
    for v in range(RANGES):
        y, core = divmod(v, 2)
        scale = scale_of(in_ref[v, TILES * ROWS : DEST, :].astype(i32).astype(f32))
        for t in range(TILES):
            column = t * ENTRY + core * HALF + y * LANES
            value = in_ref[v, t * ROWS : (t + 1) * ROWS, :].astype(i32).astype(f32)
            out_ref[:, column : column + LANES] = value * scale[t : t + 1, :]


def finish(parts):
    return pl.pallas_call(
        finish_kernel,
        out_shape=shape((ROWS, TILES * ENTRY), f32),
        in_specs=[VMEM],
        out_specs=VMEM,
        compiler_params=params(),
    )(parts)


def shards(amplitudes, tile_live, integrals, block_live, row_owner):
    packed = pack(tile_live, amplitudes)
    row = jnp.concatenate([packed] + [shift_first(packed, b) for b in range(1, RING)], 0)
    amps = {0: row, 1: shift_second(row, 1), 3: shift_second(row, 3)}
    blocks = fetch_blocks(block_live, integrals, row)
    late, amps[3], blocks = lax.optimization_barrier((row, amps[3], blocks))
    amps[2] = shift_second(late, 2)

    theirs0, mine0 = compute(0, block_live, blocks, {a: amps[a] for a in NEAR})
    other0 = shift_core(theirs0)
    theirs1, mine1 = compute(1, block_live, blocks, amps)
    other1 = shift_core(theirs1)
    own0, *sends0 = core_sum(mine0, other0)
    codes0 = [shift_y(sends0[d - 1], d) for d in range(1, RING)]
    own1, *sends1 = core_sum(mine1, other1)
    codes1 = [shift_y(sends1[d - 1], d) for d in range(1, RING)]
    parts = ring_sum(0, own0, codes0)
    parts = ring_sum(1, own1, codes1, parts)
    parts = lax.all_to_all(parts, "occ", split_axis=0, concat_axis=0, tiled=True)
    parts = reorder(row_owner, parts)
    parts = lax.all_to_all(parts, "vir", split_axis=0, concat_axis=0, tiled=True)
    return finish(parts)


def solution(mesh):
    return jax.shard_map(
        shards,
        mesh=mesh,
        in_specs=(
            P("occ", "vir"),
            P("occ", "vir"),
            P("occ", "vir", None, None),
            P("occ", "vir"),
            P(),
        ),
        out_specs=P("occ", "vir"),
        check_vma=False,
    )
```

```python
import functools

import jax
import jax.numpy as jnp
from jax import lax
from jax.experimental import pallas as pl
from jax.experimental.pallas import tpu as pltpu
from jax.sharding import PartitionSpec as P

RING = 4
TILES = 4
LIVE = 2
ROWS = 32
ENTRY = 1024
SLOTS = 2
BLOCKS = 16
LANES = 128
KB = ENTRY // LANES
META = 16
TAG = KB * LIVE * ROWS
PIECE = TAG + META
HALF = ENTRY // 2
CHUNK = 256
SIZES = (64, 128, CHUNK)
CODE = 32700.0
TINY = 1e-33

f32, bf16, i32, i16 = jnp.float32, jnp.bfloat16, jnp.int32, jnp.int16
VMEM = pl.BlockSpec(memory_space=pltpu.VMEM)
SMEM = pl.BlockSpec(memory_space=pltpu.SMEM)
HBM = pl.BlockSpec(memory_space=pltpu.HBM)
ANY = pl.BlockSpec(memory_space=pl.ANY)


def shape(dims, dtype):
    return jax.ShapeDtypeStruct(dims, dtype)


def position():
    occ, vir = lax.axis_index("occ"), lax.axis_index("vir")
    return occ // RING, lax.rem(occ, RING), vir // 2, lax.rem(vir, 2)


def in_hbm(*arrays):
    return [pltpu.with_memory_space_constraint(a, pltpu.HBM) for a in arrays]


def in_vmem(*arrays):
    return [pltpu.with_memory_space_constraint(a, pltpu.VMEM) for a in arrays]


def params(mib=4):
    return pltpu.CompilerParams(vmem_limit_bytes=mib * 1024 * 1024)


def pack_kernel(live_hbm, amp_hbm, out_ref, amp, live, sems):
    copies = (
        pltpu.make_async_copy(live_hbm, live, sems.at[0]),
        pltpu.make_async_copy(amp_hbm, amp, sems.at[1]),
    )
    for copy in copies:
        copy.start()
    for copy in copies:
        copy.wait()
    c0 = jnp.int32(0)
    for c in reversed(range(TILES)):
        c0 = jnp.where(live[0, c] != 0, c, c0)
    c1 = jnp.int32(TILES)
    for c in reversed(range(TILES)):
        c1 = jnp.where((live[0, c] != 0) & (c > c0), c, c1)
    for slot, c in enumerate((c0, jnp.minimum(c1, TILES - 1))):
        for kb in range(KB):
            start = pl.multiple_of(c * ENTRY + kb * LANES, LANES)
            out_ref[pl.ds((kb * LIVE + slot) * ROWS, ROWS), :] = amp[:, pl.ds(start, LANES)]
    tag = jnp.full((META, LANES), c0 * 8 + c1, i32)
    out_ref[pl.ds(TAG, META), :] = tag.astype(f32).astype(bf16)


def pack(tile_live, amplitudes):
    return pl.pallas_call(
        pack_kernel,
        out_shape=shape((PIECE, LANES), bf16),
        in_specs=[HBM, HBM],
        out_specs=VMEM,
        scratch_shapes=[
            pltpu.VMEM(amplitudes.shape, bf16),
            pltpu.SMEM(tile_live.shape, i32),
            pltpu.SemaphoreType.DMA((2,)),
        ],
        compiler_params=params(),
    )(*in_hbm(tile_live, amplitudes))


def shift(value, place):
    def index(x, z, y, core):
        return ((x % RING) * RING + z % RING) * 2 * RING + (y % RING) * 2 + core % 2

    spots = [(x, z, y, c) for x in range(RING) for z in range(RING) for y in range(RING) for c in range(2)]
    return lax.ppermute(value, ("occ", "vir"), [(index(*s), index(*place(*s))) for s in spots])


def shift_first(value, n):
    return shift(value, lambda x, z, y, c: (x, z + n, y, c) if c == 0 else (x + n, z, y, c))


def shift_second(value, n):
    return shift(value, lambda x, z, y, c: (x + n, z, y, c) if c == 0 else (x, z + n, y, c))


def shift_y(value, n):
    return shift(value, lambda x, z, y, c: (x, z, y + n, c))


def shift_core(value):
    return shift(value, lambda x, z, y, c: (x, z, y, c + 1))


NEAR = (0, 1, 3)
GROUPS = (
    [(e, d) for e in NEAR for d in NEAR],
    [(2, d) for d in range(RING)] + [(e, 2) for e in NEAR],
)


def compute_kernel(group, sources, fetches, live_hbm, ints_hbm, *refs):
    count_in = max(at for at, _ in sources.values()) + 1
    arrays = refs[:count_in]
    refs = refs[count_in + (0 if fetches else 1) :]
    theirs_ref, mine_ref, block_ref, left, product, table_v, table, live, count, where, sem, sems = refs
    core = position()[3]
    copy_live = pltpu.make_async_copy(live_hbm, live, sem.at[0])
    copy_live.start()

    def fetch(i):
        return pltpu.make_async_copy(ints_hbm.at[lax.rem(i, SLOTS), i // SLOTS], block_ref.at[i], sems.at[i])

    def piece(a, b, row, rows):
        at, base = sources[a, b]
        return arrays[at][pl.ds(base + row, rows), :]

    lane = lax.broadcasted_iota(i32, (8, LANES), 1)
    entries = jnp.zeros((8, LANES), i32)
    for k, (a, b) in enumerate(group):
        tag = piece(a, b, TAG, META).astype(f32)[:8].astype(i32)
        entries = jnp.where(lane == k, tag, entries)
    table_v[...] = entries
    copy_table = pltpu.make_async_copy(table_v, table, sem.at[1])
    copy_table.start()

    copy_live.wait()
    if fetches:
        for i in range(TILES * SLOTS):
            pl.when(live[i % SLOTS, i // SLOTS] != 0)(functools.partial(lambda i: fetch(i).start(), i))
    theirs_ref[...] = jnp.zeros_like(theirs_ref)
    mine_ref[...] = jnp.zeros_like(mine_ref)
    for c in range(TILES):
        count[c] = 0
    copy_table.wait()

    for k, (a, b) in enumerate(group):
        tag = table[0, k]
        o = jnp.where(core == 0, k, group.index((b, a)))
        for slot in range(LIVE):
            c = tag // 8 if slot == 0 else lax.rem(tag, 8)

            @pl.when(c < TILES)
            def _():
                at = count[c]
                count[c] = at + 1
                where[c * BLOCKS + at] = o
                rows = pl.multiple_of(at * ROWS, ROWS)
                for kb in range(KB):
                    left[c, pl.ds(rows, ROWS), kb * LANES : (kb + 1) * LANES] = piece(
                        a, b, (kb * LIVE + slot) * ROWS, ROWS
                    )

    def one_block(i, carry):
        c, r = i // SLOTS, lax.rem(i, SLOTS)

        @pl.when(live[r, c] != 0)
        def _():
            if fetches:
                fetch(i).wait()
            n = count[c]

            def one_chunk(j, inner):
                rest = n - j * (CHUNK // ROWS)
                start = pl.multiple_of(j * CHUNK, CHUNK)

                def multiply(rows):
                    product[:rows, :] = jnp.dot(
                        left[c, pl.ds(start, rows), :], block_ref[i], preferred_element_type=f32
                    )

                low = 0
                for rows in SIZES:
                    tiles = rows // ROWS
                    pl.when((rest > low) & ((rest <= tiles) | (rows == CHUNK)))(functools.partial(multiply, rows))
                    low = tiles

                def add(t, last):
                    o = where[c * BLOCKS + j * (CHUNK // ROWS) + t]
                    rows = pl.ds(pl.multiple_of(t * ROWS, ROWS), ROWS)
                    at = pl.ds(pl.multiple_of((o * SLOTS + r) * ROWS, ROWS), ROWS)
                    for part, ref in enumerate((mine_ref, theirs_ref)):
                        start = pl.multiple_of(jnp.where(core == 0, part, 1 - part) * HALF, HALF)
                        for q in range(RING):
                            ref[q, at, :] += product[rows, pl.ds(start + q * LANES, LANES)]
                    return last

                lax.fori_loop(0, jnp.minimum(rest, CHUNK // ROWS), add, 0)
                return inner

            lax.fori_loop(0, pl.cdiv(n * ROWS, CHUNK), one_chunk, 0)

        return carry

    lax.fori_loop(0, TILES * SLOTS, one_block, 0)


def compute(which, block_live, integrals, blocks, pieces):
    group = GROUPS[which]
    fetches = blocks is None
    sources = {ab: (i, k * PIECE) for i, (_, held) in enumerate(pieces) for k, ab in enumerate(held)}
    total = pltpu.VMEM((RING, len(group) * SLOTS * ROWS, LANES), f32)
    more = [] if fetches else in_vmem(blocks)
    return pl.pallas_call(
        functools.partial(compute_kernel, group, sources, fetches),
        out_shape=(total, total, pltpu.VMEM((TILES * SLOTS, ENTRY, ENTRY), bf16)),
        in_specs=[HBM, HBM] + [VMEM] * (len(pieces) + len(more)),
        out_specs=(VMEM,) * 3,
        input_output_aliases={} if fetches else {2 + len(pieces): 2},
        scratch_shapes=[
            pltpu.VMEM((TILES, 2 * CHUNK, ENTRY), bf16),
            pltpu.VMEM((CHUNK, ENTRY), f32),
            pltpu.VMEM((8, LANES), i32),
            pltpu.SMEM((8, LANES), i32),
            pltpu.SMEM(block_live.shape, i32),
            pltpu.SMEM((TILES,), i32),
            pltpu.SMEM((TILES * BLOCKS,), i32),
            pltpu.SemaphoreType.DMA((2,)),
            pltpu.SemaphoreType.DMA((TILES * SLOTS,)),
        ],
        compiler_params=params(8),
        cost_estimate=pl.CostEstimate(flops=1 << 32, bytes_accessed=8 << 20, transcendentals=0),
    )(*in_hbm(block_live, integrals), *[array for array, _ in pieces], *more)


def encode(value):
    top = jnp.maximum(jnp.max(jnp.abs(value), axis=0, keepdims=True), TINY)
    exponent = jnp.ceil(jnp.log(top) * (8.0 / 0.6931471805599453) + 0.01)
    inverse = jnp.exp(exponent * (-0.6931471805599453 / 8.0)) * CODE
    return jnp.round(value * inverse).astype(i32).astype(i16), exponent


def scale_of(exponent):
    return jnp.exp(exponent * (0.6931471805599453 / 8.0)) * (1.0 / CODE)


def tag_rows(sums):
    return pl.cdiv(sums, META) * META


def core_sum_kernel(mine_ref, other_ref, own_ref, *refs):
    sends, exps = refs[: RING - 1], refs[RING - 1]
    y = position()[2]
    rows = own_ref.shape[0]
    own_ref[...] = mine_ref[y] + other_ref[y]
    exps[...] = jnp.zeros_like(exps)
    for d in range(1, RING):
        q = lax.rem(y + d, RING)

        def group(g, carry):
            at = pl.ds(pl.multiple_of(g * ROWS, ROWS), ROWS)
            codes, exponent = encode(mine_ref[q, at, :] + other_ref[q, at, :])
            sends[d - 1][at, :] = codes
            exps[pl.ds(g, 1), :] = exponent
            return carry

        lax.fori_loop(0, rows // ROWS, group, 0, unroll=2)
        sends[d - 1][pl.ds(rows, exps.shape[0]), :] = exps[...].astype(i32).astype(i16)


def core_sum(mine, other):
    rows = mine.shape[1]
    tags = tag_rows(rows // ROWS)
    code = shape((rows + tags, LANES), i16)
    return pl.pallas_call(
        core_sum_kernel,
        out_shape=(shape((rows, LANES), f32), code, code, code),
        in_specs=[VMEM, VMEM],
        out_specs=(VMEM,) * RING,
        scratch_shapes=[pltpu.VMEM((tags, LANES), f32)],
        compiler_params=params(),
    )(mine, other)


PART = SLOTS * ROWS + META


def ring_sum_kernel(group, own_ref, a_ref, b_ref, c_ref, *refs):
    out_ref, scales, exps = refs[-3:]
    x, z = position()[:2]
    codes = (a_ref, b_ref, c_ref)
    rows, tags = own_ref.shape[0], scales.shape[1]
    for k in range(RING - 1):
        scales[k] = scale_of(codes[k][pl.ds(rows, tags), :].astype(i32).astype(f32))
    exps[...] = jnp.zeros_like(exps)
    for o, (e, d) in enumerate(group):
        to = lax.rem(x - e + RING, RING) * RING + lax.rem(z - d + RING, RING)
        for r in range(SLOTS):
            g = o * SLOTS + r
            at = pl.ds(g * ROWS, ROWS)
            total = own_ref[at, :]
            for k in range(RING - 1):
                total += codes[k][at, :].astype(i32).astype(f32) * scales[k, g : g + 1, :]
            code, exponent = encode(total)
            out_ref[to, r * ROWS : (r + 1) * ROWS, :] = code
            exps[r : r + 1, :] = exponent
        out_ref[to, SLOTS * ROWS : PART, :] = exps[...].astype(i32).astype(i16)


def ring_sum(which, own, codes, parts=None):
    more = [] if parts is None else [parts]
    return pl.pallas_call(
        functools.partial(ring_sum_kernel, GROUPS[which]),
        out_shape=shape((BLOCKS, PART, LANES), i16),
        in_specs=[VMEM] * (RING + len(more)),
        out_specs=VMEM,
        input_output_aliases={RING: 0} if more else {},
        scratch_shapes=[
            pltpu.VMEM((RING - 1, tag_rows(own.shape[0] // ROWS), LANES), f32),
            pltpu.VMEM((META, LANES), f32),
        ],
        compiler_params=params(),
    )(own, *codes, *more)


RANGES = 8
DEST = TILES * ROWS + META


def reorder_kernel(owner_ref, in_ref, out_ref, exps):
    for s in range(BLOCKS * SLOTS):
        owner, r = divmod(s, SLOTS)
        p = owner_ref[s]
        v, t = p // TILES, lax.rem(p, TILES)
        out_ref[v, pl.ds(pl.multiple_of(t * ROWS, ROWS), ROWS), :] = in_ref[owner, r * ROWS : (r + 1) * ROWS, :]
        tags = in_ref[owner, SLOTS * ROWS : PART, :].astype(i32).astype(f32)
        exps[pl.ds(v * META + t, 1), :] = tags[r : r + 1, :]
    for v in range(RANGES):
        out_ref[v, TILES * ROWS : DEST, :] = exps[v * META : (v + 1) * META, :].astype(i32).astype(i16)


def reorder(row_owner, parts):
    return pl.pallas_call(
        reorder_kernel,
        out_shape=shape((RANGES, DEST, LANES), i16),
        in_specs=[SMEM, VMEM],
        out_specs=VMEM,
        scratch_shapes=[pltpu.VMEM((RANGES * META, LANES), f32)],
        compiler_params=params(),
    )(row_owner, parts)


def finish_kernel(in_ref, out_ref):
    for v in range(RANGES):
        y, core = divmod(v, 2)
        scale = scale_of(in_ref[v, TILES * ROWS : DEST, :].astype(i32).astype(f32))
        for t in range(TILES):
            column = t * ENTRY + core * HALF + y * LANES
            value = in_ref[v, t * ROWS : (t + 1) * ROWS, :].astype(i32).astype(f32)
            out_ref[:, column : column + LANES] = value * scale[t : t + 1, :]


def finish(parts):
    return pl.pallas_call(
        finish_kernel,
        out_shape=shape((ROWS, TILES * ENTRY), f32),
        in_specs=[VMEM],
        out_specs=VMEM,
        compiler_params=params(),
    )(parts)


def shards(amplitudes, tile_live, integrals, block_live, row_owner):
    own = pack(tile_live, amplitudes)
    by1, by3, by2 = (shift_first(own, b) for b in (1, 3, 2))
    at_once = {a: shift_second(own, a) for a in (1, 3)}
    near = jnp.concatenate([by1, by3], 0)
    nears = {a: shift_second(near, a) for a in (1, 3)}
    row = jnp.concatenate([own, by1, by2, by3], 0)
    row, nears[3] = lax.optimization_barrier((row, nears[3]))
    first = [(own, [(0, 0)]), (by1, [(0, 1)]), (by3, [(0, 3)])]
    for a in (1, 3):
        first += [(at_once[a], [(a, 0)]), (nears[a], [(a, 1), (a, 3)])]
    second = [(shift_second(row, 2), [(2, b) for b in range(RING)]), (by2, [(0, 2)])]
    second += [(shift_second(by2, a), [(a, 2)]) for a in (1, 3)]

    theirs0, mine0, blocks = compute(0, block_live, integrals, None, first)
    other0 = shift_core(theirs0)
    theirs1, mine1, _ = compute(1, block_live, integrals, blocks, second)
    other1 = shift_core(theirs1)
    own0, *sends0 = core_sum(mine0, other0)
    codes0 = [shift_y(sends0[d - 1], d) for d in range(1, RING)]
    own1, *sends1 = core_sum(mine1, other1)
    codes1 = [shift_y(sends1[d - 1], d) for d in range(1, RING)]
    parts = ring_sum(0, own0, codes0)
    parts = ring_sum(1, own1, codes1, parts)
    parts = lax.all_to_all(parts, "occ", split_axis=0, concat_axis=0, tiled=True)
    parts = reorder(row_owner, parts)
    parts = lax.all_to_all(parts, "vir", split_axis=0, concat_axis=0, tiled=True)
    return finish(parts)


def solution(mesh):
    return jax.shard_map(
        shards,
        mesh=mesh,
        in_specs=(
            P("occ", "vir"),
            P("occ", "vir"),
            P("occ", "vir", None, None),
            P("occ", "vir"),
            P(),
        ),
        out_specs=P("occ", "vir"),
        check_vma=False,
    )
```

```python
import functools

import jax
import jax.numpy as jnp
from jax import lax
from jax.experimental import pallas as pl
from jax.experimental.pallas import tpu as pltpu
from jax.sharding import PartitionSpec as P

RING = 4
TILES = 4
LIVE = 2
ROWS = 32
ENTRY = 1024
SLOTS = 2
BLOCKS = 16
LANES = 128
KB = ENTRY // LANES
META = 16
TAG = KB * LIVE * ROWS
PIECE = TAG + META
HALF = ENTRY // 2
CHUNK = 256
SIZES = (64, 128, CHUNK)
EARLY = 4
CODE = 32700.0
TINY = 1e-33

f32, bf16, i32, i16 = jnp.float32, jnp.bfloat16, jnp.int32, jnp.int16
VMEM = pl.BlockSpec(memory_space=pltpu.VMEM)
SMEM = pl.BlockSpec(memory_space=pltpu.SMEM)
HBM = pl.BlockSpec(memory_space=pltpu.HBM)
ANY = pl.BlockSpec(memory_space=pl.ANY)


def shape(dims, dtype):
    return jax.ShapeDtypeStruct(dims, dtype)


def position():
    occ, vir = lax.axis_index("occ"), lax.axis_index("vir")
    return occ // RING, lax.rem(occ, RING), vir // 2, lax.rem(vir, 2)


def in_hbm(*arrays):
    return [pltpu.with_memory_space_constraint(a, pltpu.HBM) for a in arrays]


def in_vmem(*arrays):
    return [pltpu.with_memory_space_constraint(a, pltpu.VMEM) for a in arrays]


def params(mib=4):
    return pltpu.CompilerParams(vmem_limit_bytes=mib * 1024 * 1024)


def pack_kernel(live_hbm, amp_hbm, out_ref, amp, live, sems):
    copies = (
        pltpu.make_async_copy(live_hbm, live, sems.at[0]),
        pltpu.make_async_copy(amp_hbm, amp, sems.at[1]),
    )
    for copy in copies:
        copy.start()
    for copy in copies:
        copy.wait()
    c0 = jnp.int32(0)
    for c in reversed(range(TILES)):
        c0 = jnp.where(live[0, c] != 0, c, c0)
    c1 = jnp.int32(TILES)
    for c in reversed(range(TILES)):
        c1 = jnp.where((live[0, c] != 0) & (c > c0), c, c1)
    for slot, c in enumerate((c0, jnp.minimum(c1, TILES - 1))):
        for kb in range(KB):
            start = pl.multiple_of(c * ENTRY + kb * LANES, LANES)
            out_ref[pl.ds((kb * LIVE + slot) * ROWS, ROWS), :] = amp[:, pl.ds(start, LANES)]
    tag = jnp.full((META, LANES), c0 * 8 + c1, i32)
    out_ref[pl.ds(TAG, META), :] = tag.astype(f32).astype(bf16)


def pack(tile_live, amplitudes):
    return pl.pallas_call(
        pack_kernel,
        out_shape=shape((PIECE, LANES), bf16),
        in_specs=[HBM, HBM],
        out_specs=VMEM,
        scratch_shapes=[
            pltpu.VMEM(amplitudes.shape, bf16),
            pltpu.SMEM(tile_live.shape, i32),
            pltpu.SemaphoreType.DMA((2,)),
        ],
        compiler_params=params(),
    )(*in_hbm(tile_live, amplitudes))


def shift(value, place):
    def index(x, z, y, core):
        return ((x % RING) * RING + z % RING) * 2 * RING + (y % RING) * 2 + core % 2

    spots = [(x, z, y, c) for x in range(RING) for z in range(RING) for y in range(RING) for c in range(2)]
    return lax.ppermute(value, ("occ", "vir"), [(index(*s), index(*place(*s))) for s in spots])


def shift_first(value, n):
    return shift(value, lambda x, z, y, c: (x, z + n, y, c) if c == 0 else (x + n, z, y, c))


def shift_second(value, n):
    return shift(value, lambda x, z, y, c: (x + n, z, y, c) if c == 0 else (x, z + n, y, c))


def shift_y(value, n):
    return shift(value, lambda x, z, y, c: (x, z, y + n, c))


def shift_core(value):
    return shift(value, lambda x, z, y, c: (x, z, y, c + 1))


def fetch_kernel(live_hbm, ints_hbm, after_ref, block_ref, live, sem, sems):
    del after_ref
    copy = pltpu.make_async_copy(live_hbm, live, sem)
    copy.start()
    copy.wait()

    def fetch(i):
        return pltpu.make_async_copy(ints_hbm.at[i % SLOTS, i // SLOTS], block_ref.at[i], sems.at[i])

    for i in range(EARLY):
        pl.when(live[i % SLOTS, i // SLOTS] != 0)(functools.partial(lambda i: fetch(i).start(), i))
    for i in range(EARLY):
        pl.when(live[i % SLOTS, i // SLOTS] != 0)(functools.partial(lambda i: fetch(i).wait(), i))


def fetch_blocks(block_live, integrals, after):
    return pl.pallas_call(
        fetch_kernel,
        out_shape=pltpu.VMEM((TILES * SLOTS, ENTRY, ENTRY), bf16),
        in_specs=[HBM, HBM, ANY],
        out_specs=VMEM,
        scratch_shapes=[
            pltpu.SMEM(block_live.shape, i32),
            pltpu.SemaphoreType.DMA,
            pltpu.SemaphoreType.DMA((EARLY,)),
        ],
        compiler_params=params(2),
        cost_estimate=pl.CostEstimate(flops=0, bytes_accessed=16 << 20, transcendentals=0),
    )(*in_hbm(block_live, integrals), after)


NEAR = (0, 1, 3)
GROUPS = (
    [(e, d) for e in NEAR for d in NEAR],
    [(2, d) for d in range(RING)] + [(e, 2) for e in NEAR],
)


def compute_kernel(group, sources, fetches, live_hbm, ints_hbm, *refs):
    count_in = max(at for at, _ in sources.values()) + 1
    arrays = refs[:count_in]
    refs = refs[count_in + 1 :]
    theirs_ref, mine_ref, block_ref, left, product, table_v, table, live, count, where, sem, sems = refs
    core = position()[3]
    copy_live = pltpu.make_async_copy(live_hbm, live, sem.at[0])
    copy_live.start()

    def fetch(i):
        return pltpu.make_async_copy(ints_hbm.at[lax.rem(i, SLOTS), i // SLOTS], block_ref.at[i], sems.at[i])

    def piece(a, b, row, rows):
        at, base = sources[a, b]
        return arrays[at][pl.ds(base + row, rows), :]

    lane = lax.broadcasted_iota(i32, (8, LANES), 1)
    entries = jnp.zeros((8, LANES), i32)
    for k, (a, b) in enumerate(group):
        tag = piece(a, b, TAG, META).astype(f32)[:8].astype(i32)
        entries = jnp.where(lane == k, tag, entries)
    table_v[...] = entries
    copy_table = pltpu.make_async_copy(table_v, table, sem.at[1])
    copy_table.start()

    copy_live.wait()
    if fetches:
        for i in range(EARLY, TILES * SLOTS):
            pl.when(live[i % SLOTS, i // SLOTS] != 0)(functools.partial(lambda i: fetch(i).start(), i))
    theirs_ref[...] = jnp.zeros_like(theirs_ref)
    mine_ref[...] = jnp.zeros_like(mine_ref)
    for c in range(TILES):
        count[c] = 0
    copy_table.wait()

    for k, (a, b) in enumerate(group):
        tag = table[0, k]
        o = jnp.where(core == 0, k, group.index((b, a)))
        for slot in range(LIVE):
            c = tag // 8 if slot == 0 else lax.rem(tag, 8)

            @pl.when(c < TILES)
            def _():
                at = count[c]
                count[c] = at + 1
                where[c * BLOCKS + at] = o
                rows = pl.multiple_of(at * ROWS, ROWS)
                for kb in range(KB):
                    left[c, pl.ds(rows, ROWS), kb * LANES : (kb + 1) * LANES] = piece(
                        a, b, (kb * LIVE + slot) * ROWS, ROWS
                    )

    def one_block(i, carry):
        c, r = i // SLOTS, lax.rem(i, SLOTS)

        @pl.when(live[r, c] != 0)
        def _():
            if fetches:
                pl.when(i >= EARLY)(lambda: fetch(i).wait())
            n = count[c]

            def one_chunk(j, inner):
                rest = n - j * (CHUNK // ROWS)
                start = pl.multiple_of(j * CHUNK, CHUNK)

                def multiply(rows):
                    product[:rows, :] = jnp.dot(
                        left[c, pl.ds(start, rows), :], block_ref[i], preferred_element_type=f32
                    )

                low = 0
                for rows in SIZES:
                    tiles = rows // ROWS
                    pl.when((rest > low) & ((rest <= tiles) | (rows == CHUNK)))(functools.partial(multiply, rows))
                    low = tiles

                def add(t, last):
                    o = where[c * BLOCKS + j * (CHUNK // ROWS) + t]
                    rows = pl.ds(pl.multiple_of(t * ROWS, ROWS), ROWS)
                    at = pl.ds(pl.multiple_of((o * SLOTS + r) * ROWS, ROWS), ROWS)
                    for part, ref in enumerate((mine_ref, theirs_ref)):
                        start = pl.multiple_of(jnp.where(core == 0, part, 1 - part) * HALF, HALF)
                        for q in range(RING):
                            ref[q, at, :] += product[rows, pl.ds(start + q * LANES, LANES)]
                    return last

                lax.fori_loop(0, jnp.minimum(rest, CHUNK // ROWS), add, 0)
                return inner

            lax.fori_loop(0, pl.cdiv(n * ROWS, CHUNK), one_chunk, 0)

        return carry

    lax.fori_loop(0, TILES * SLOTS, one_block, 0)


def compute(which, block_live, integrals, blocks, pieces):
    group = GROUPS[which]
    fetches = which == 0
    sources = {ab: (i, k * PIECE) for i, (_, held) in enumerate(pieces) for k, ab in enumerate(held)}
    total = pltpu.VMEM((RING, len(group) * SLOTS * ROWS, LANES), f32)
    more = in_vmem(blocks)
    return pl.pallas_call(
        functools.partial(compute_kernel, group, sources, fetches),
        out_shape=(total, total, pltpu.VMEM((TILES * SLOTS, ENTRY, ENTRY), bf16)),
        in_specs=[HBM, HBM] + [VMEM] * (len(pieces) + len(more)),
        out_specs=(VMEM,) * 3,
        input_output_aliases={2 + len(pieces): 2},
        scratch_shapes=[
            pltpu.VMEM((TILES, 2 * CHUNK, ENTRY), bf16),
            pltpu.VMEM((CHUNK, ENTRY), f32),
            pltpu.VMEM((8, LANES), i32),
            pltpu.SMEM((8, LANES), i32),
            pltpu.SMEM(block_live.shape, i32),
            pltpu.SMEM((TILES,), i32),
            pltpu.SMEM((TILES * BLOCKS,), i32),
            pltpu.SemaphoreType.DMA((2,)),
            pltpu.SemaphoreType.DMA((TILES * SLOTS,)),
        ],
        compiler_params=params(8),
        cost_estimate=pl.CostEstimate(flops=1 << 32, bytes_accessed=8 << 20, transcendentals=0),
    )(*in_hbm(block_live, integrals), *[array for array, _ in pieces], *more)


def encode(value):
    top = jnp.maximum(jnp.max(jnp.abs(value), axis=0, keepdims=True), TINY)
    exponent = jnp.ceil(jnp.log(top) * (8.0 / 0.6931471805599453) + 0.01)
    inverse = jnp.exp(exponent * (-0.6931471805599453 / 8.0)) * CODE
    return jnp.round(value * inverse).astype(i32).astype(i16), exponent


def scale_of(exponent):
    return jnp.exp(exponent * (0.6931471805599453 / 8.0)) * (1.0 / CODE)


def tag_rows(sums):
    return pl.cdiv(sums, META) * META


def core_sum_kernel(mine_ref, other_ref, own_ref, *refs):
    sends, exps = refs[: RING - 1], refs[RING - 1]
    y = position()[2]
    rows = own_ref.shape[0]
    own_ref[...] = mine_ref[y] + other_ref[y]
    exps[...] = jnp.zeros_like(exps)
    for d in range(1, RING):
        q = lax.rem(y + d, RING)

        for g in range(rows // ROWS):
            at = pl.ds(g * ROWS, ROWS)
            codes, exponent = encode(mine_ref[q, at, :] + other_ref[q, at, :])
            sends[d - 1][at, :] = codes
            exps[g : g + 1, :] = exponent
        sends[d - 1][pl.ds(rows, exps.shape[0]), :] = exps[...].astype(i32).astype(i16)


def core_sum(mine, other):
    rows = mine.shape[1]
    tags = tag_rows(rows // ROWS)
    code = shape((rows + tags, LANES), i16)
    return pl.pallas_call(
        core_sum_kernel,
        out_shape=(shape((rows, LANES), f32), code, code, code),
        in_specs=[VMEM, VMEM],
        out_specs=(VMEM,) * RING,
        scratch_shapes=[pltpu.VMEM((tags, LANES), f32)],
        compiler_params=params(),
    )(mine, other)


PART = SLOTS * ROWS + META


def ring_sum_kernel(group, own_ref, a_ref, b_ref, c_ref, *refs):
    out_ref, scales, exps = refs[-3:]
    x, z = position()[:2]
    codes = (a_ref, b_ref, c_ref)
    rows, tags = own_ref.shape[0], scales.shape[1]
    for k in range(RING - 1):
        scales[k] = scale_of(codes[k][pl.ds(rows, tags), :].astype(i32).astype(f32))
    exps[...] = jnp.zeros_like(exps)
    for o, (e, d) in enumerate(group):
        to = lax.rem(x - e + RING, RING) * RING + lax.rem(z - d + RING, RING)
        for r in range(SLOTS):
            g = o * SLOTS + r
            at = pl.ds(g * ROWS, ROWS)
            total = own_ref[at, :]
            for k in range(RING - 1):
                total += codes[k][at, :].astype(i32).astype(f32) * scales[k, g : g + 1, :]
            code, exponent = encode(total)
            out_ref[to, r * ROWS : (r + 1) * ROWS, :] = code
            exps[r : r + 1, :] = exponent
        out_ref[to, SLOTS * ROWS : PART, :] = exps[...].astype(i32).astype(i16)


def ring_sum(which, own, codes, parts=None):
    more = [] if parts is None else [parts]
    return pl.pallas_call(
        functools.partial(ring_sum_kernel, GROUPS[which]),
        out_shape=shape((BLOCKS, PART, LANES), i16),
        in_specs=[VMEM] * (RING + len(more)),
        out_specs=VMEM,
        input_output_aliases={RING: 0} if more else {},
        scratch_shapes=[
            pltpu.VMEM((RING - 1, tag_rows(own.shape[0] // ROWS), LANES), f32),
            pltpu.VMEM((META, LANES), f32),
        ],
        compiler_params=params(),
    )(own, *codes, *more)


RANGES = 8
DEST = TILES * ROWS + META


def reorder_kernel(owner_ref, in_ref, out_ref, exps):
    for owner in range(BLOCKS):
        tags = in_ref[owner, SLOTS * ROWS : PART, :].astype(i32).astype(f32)
        for r in range(SLOTS):
            p = owner_ref[owner * SLOTS + r]
            v, t = p // TILES, lax.rem(p, TILES)
            rows = pl.ds(pl.multiple_of(t * ROWS, ROWS), ROWS)
            out_ref[v, rows, :] = in_ref[owner, r * ROWS : (r + 1) * ROWS, :]
            exps[pl.ds(v * META + t, 1), :] = tags[r : r + 1, :]
    for v in range(RANGES):
        out_ref[v, TILES * ROWS : DEST, :] = exps[v * META : (v + 1) * META, :].astype(i32).astype(i16)


def reorder(row_owner, parts):
    return pl.pallas_call(
        reorder_kernel,
        out_shape=shape((RANGES, DEST, LANES), i16),
        in_specs=[SMEM, VMEM],
        out_specs=VMEM,
        scratch_shapes=[pltpu.VMEM((RANGES * META, LANES), f32)],
        compiler_params=params(),
    )(row_owner, parts)


def finish_kernel(in_ref, out_ref):
    for v in range(RANGES):
        y, core = divmod(v, 2)
        scale = scale_of(in_ref[v, TILES * ROWS : DEST, :].astype(i32).astype(f32))
        for t in range(TILES):
            column = t * ENTRY + core * HALF + y * LANES
            value = in_ref[v, t * ROWS : (t + 1) * ROWS, :].astype(i32).astype(f32)
            out_ref[:, column : column + LANES] = value * scale[t : t + 1, :]


def finish(parts):
    return pl.pallas_call(
        finish_kernel,
        out_shape=shape((ROWS, TILES * ENTRY), f32),
        in_specs=[VMEM],
        out_specs=VMEM,
        compiler_params=params(),
    )(parts)


def shards(amplitudes, tile_live, integrals, block_live, row_owner):
    own = pack(tile_live, amplitudes)
    by1, by3, by2 = (shift_first(own, b) for b in (1, 3, 2))
    at_once = {a: shift_second(own, a) for a in (1, 3)}
    near = jnp.concatenate([by1, by3], 0)
    nears = {a: shift_second(near, a) for a in (1, 3)}
    far = shift_first(jnp.concatenate([at_once[1], at_once[3]], 0), 2)
    row = jnp.concatenate([own, by1, by2, by3], 0)
    blocks = fetch_blocks(block_live, integrals, near)
    row, blocks = lax.optimization_barrier((row, blocks))
    first = [(own, [(0, 0)]), (by1, [(0, 1)]), (by3, [(0, 3)])]
    for a in (1, 3):
        first += [(at_once[a], [(a, 0)]), (nears[a], [(a, 1), (a, 3)])]
    second = [(shift_second(row, 2), [(2, b) for b in range(RING)]), (by2, [(0, 2)])]
    second += [(far, [(1, 2), (3, 2)])]

    theirs0, mine0, blocks = compute(0, block_live, integrals, blocks, first)
    other0 = shift_core(theirs0)
    theirs1, mine1, _ = compute(1, block_live, integrals, blocks, second)
    other1 = shift_core(theirs1)
    own0, *sends0 = core_sum(mine0, other0)
    codes0 = [shift_y(sends0[d - 1], d) for d in range(1, RING)]
    own1, *sends1 = core_sum(mine1, other1)
    codes1 = [shift_y(sends1[d - 1], d) for d in range(1, RING)]
    parts = ring_sum(0, own0, codes0)
    parts = ring_sum(1, own1, codes1, parts)
    parts = lax.all_to_all(parts, "occ", split_axis=0, concat_axis=0, tiled=True)
    parts = reorder(row_owner, parts)
    parts = lax.all_to_all(parts, "vir", split_axis=0, concat_axis=0, tiled=True)
    return finish(parts)


def solution(mesh):
    return jax.shard_map(
        shards,
        mesh=mesh,
        in_specs=(
            P("occ", "vir"),
            P("occ", "vir"),
            P("occ", "vir", None, None),
            P("occ", "vir"),
            P(),
        ),
        out_specs=P("occ", "vir"),
        check_vma=False,
    )
```

```python
import functools

import jax
import jax.numpy as jnp
from jax import lax
from jax.experimental import pallas as pl
from jax.experimental.pallas import tpu as pltpu
from jax.sharding import PartitionSpec as P

RING = 4
TILES = 4
LIVE = 2
ROWS = 32
ENTRY = 1024
SLOTS = 2
BLOCKS = 16
LANES = 128
KB = ENTRY // LANES
META = 16
TAG = KB * LIVE * ROWS
PIECE = TAG + META
HALF = ENTRY // 2
CHUNK = 256
SIZES = (64, 128, CHUNK)
WIDE = 512
EARLY = 4
CODE = 32700.0
TINY = 1e-33

f32, bf16, i32, i16 = jnp.float32, jnp.bfloat16, jnp.int32, jnp.int16
VMEM = pl.BlockSpec(memory_space=pltpu.VMEM)
SMEM = pl.BlockSpec(memory_space=pltpu.SMEM)
HBM = pl.BlockSpec(memory_space=pltpu.HBM)
ANY = pl.BlockSpec(memory_space=pl.ANY)


def shape(dims, dtype):
    return jax.ShapeDtypeStruct(dims, dtype)


def position():
    occ, vir = lax.axis_index("occ"), lax.axis_index("vir")
    return occ // RING, lax.rem(occ, RING), vir // 2, lax.rem(vir, 2)


def in_hbm(*arrays):
    return [pltpu.with_memory_space_constraint(a, pltpu.HBM) for a in arrays]


def in_vmem(*arrays):
    return [pltpu.with_memory_space_constraint(a, pltpu.VMEM) for a in arrays]


def params(mib=4):
    return pltpu.CompilerParams(vmem_limit_bytes=mib * 1024 * 1024)


def pack_kernel(live_hbm, amp_hbm, out_ref, amp, live, sems):
    copies = (
        pltpu.make_async_copy(live_hbm, live, sems.at[0]),
        pltpu.make_async_copy(amp_hbm, amp, sems.at[1]),
    )
    for copy in copies:
        copy.start()
    for copy in copies:
        copy.wait()
    c0 = jnp.int32(0)
    for c in reversed(range(TILES)):
        c0 = jnp.where(live[0, c] != 0, c, c0)
    c1 = jnp.int32(TILES)
    for c in reversed(range(TILES)):
        c1 = jnp.where((live[0, c] != 0) & (c > c0), c, c1)
    for slot, c in enumerate((c0, jnp.minimum(c1, TILES - 1))):
        for kb in range(KB):
            start = pl.multiple_of(c * ENTRY + kb * LANES, LANES)
            out_ref[pl.ds((kb * LIVE + slot) * ROWS, ROWS), :] = amp[:, pl.ds(start, LANES)]
    tag = jnp.full((META, LANES), c0 * 8 + c1, i32)
    out_ref[pl.ds(TAG, META), :] = tag.astype(f32).astype(bf16)


def pack(tile_live, amplitudes):
    return pl.pallas_call(
        pack_kernel,
        out_shape=shape((PIECE, LANES), bf16),
        in_specs=[HBM, HBM],
        out_specs=VMEM,
        scratch_shapes=[
            pltpu.VMEM(amplitudes.shape, bf16),
            pltpu.SMEM(tile_live.shape, i32),
            pltpu.SemaphoreType.DMA((2,)),
        ],
        compiler_params=params(),
    )(*in_hbm(tile_live, amplitudes))


def shift(value, place):
    def index(x, z, y, core):
        return ((x % RING) * RING + z % RING) * 2 * RING + (y % RING) * 2 + core % 2

    spots = [(x, z, y, c) for x in range(RING) for z in range(RING) for y in range(RING) for c in range(2)]
    return lax.ppermute(value, ("occ", "vir"), [(index(*s), index(*place(*s))) for s in spots])


def shift_first(value, n):
    return shift(value, lambda x, z, y, c: (x, z + n, y, c) if c == 0 else (x + n, z, y, c))


def shift_second(value, n):
    return shift(value, lambda x, z, y, c: (x + n, z, y, c) if c == 0 else (x, z + n, y, c))


def shift_y(value, n):
    return shift(value, lambda x, z, y, c: (x, z, y + n, c))


def shift_core(value):
    return shift(value, lambda x, z, y, c: (x, z, y, c + 1))


def fetch_kernel(live_hbm, ints_hbm, owner_hbm, after_ref, block_ref, owner_ref, live, sem, sems):
    del after_ref
    copy = pltpu.make_async_copy(live_hbm, live, sem.at[0])
    copy.start()
    copy_owner = pltpu.make_async_copy(owner_hbm, owner_ref, sem.at[1])
    copy_owner.start()
    copy.wait()

    def fetch(i):
        return pltpu.make_async_copy(ints_hbm.at[i % SLOTS, i // SLOTS], block_ref.at[i], sems.at[i])

    for i in range(EARLY):
        pl.when(live[i % SLOTS, i // SLOTS] != 0)(functools.partial(lambda i: fetch(i).start(), i))
    for i in range(EARLY):
        pl.when(live[i % SLOTS, i // SLOTS] != 0)(functools.partial(lambda i: fetch(i).wait(), i))
    copy_owner.wait()


def fetch_blocks(block_live, integrals, row_owner, after):
    return pl.pallas_call(
        fetch_kernel,
        out_shape=(pltpu.VMEM((TILES * SLOTS, ENTRY, ENTRY), bf16), pltpu.SMEM(row_owner.shape, i32)),
        in_specs=[HBM, HBM, HBM, ANY],
        out_specs=(VMEM, SMEM),
        scratch_shapes=[
            pltpu.SMEM(block_live.shape, i32),
            pltpu.SemaphoreType.DMA((2,)),
            pltpu.SemaphoreType.DMA((EARLY,)),
        ],
        compiler_params=params(2),
        cost_estimate=pl.CostEstimate(flops=0, bytes_accessed=16 << 20, transcendentals=0),
    )(*in_hbm(block_live, integrals, row_owner), after)


NEAR = (0, 1, 3)
GROUPS = (
    [(e, d) for e in NEAR for d in NEAR],
    [(2, d) for d in range(RING)] + [(e, 2) for e in NEAR],
)


def compute_kernel(group, sources, fetches, live_hbm, ints_hbm, *refs):
    count_in = max(at for at, _ in sources.values()) + 1
    arrays = refs[:count_in]
    refs = refs[count_in + 1 :]
    theirs_ref, mine_ref, block_ref, left, table_v, table, live, count, where, sem, sems = refs
    core = position()[3]
    copy_live = pltpu.make_async_copy(live_hbm, live, sem.at[0])
    copy_live.start()

    def fetch(i):
        return pltpu.make_async_copy(ints_hbm.at[lax.rem(i, SLOTS), i // SLOTS], block_ref.at[i], sems.at[i])

    def piece(a, b, row, rows):
        at, base = sources[a, b]
        return arrays[at][pl.ds(base + row, rows), :]

    lane = lax.broadcasted_iota(i32, (8, LANES), 1)
    entries = jnp.zeros((8, LANES), i32)
    for k, (a, b) in enumerate(group):
        tag = piece(a, b, TAG, META).astype(f32)[:8].astype(i32)
        entries = jnp.where(lane == k, tag, entries)
    table_v[...] = entries
    copy_table = pltpu.make_async_copy(table_v, table, sem.at[1])
    copy_table.start()

    copy_live.wait()
    if fetches:
        for i in range(EARLY, TILES * SLOTS):
            pl.when(live[i % SLOTS, i // SLOTS] != 0)(functools.partial(lambda i: fetch(i).start(), i))
    theirs_ref[...] = jnp.zeros_like(theirs_ref)
    mine_ref[...] = jnp.zeros_like(mine_ref)
    for c in range(TILES):
        count[c] = 0
    copy_table.wait()

    for k, (a, b) in enumerate(group):
        tag = table[0, k]
        o = jnp.where(core == 0, k, group.index((b, a)))
        for slot in range(LIVE):
            c = tag // 8 if slot == 0 else lax.rem(tag, 8)

            @pl.when(c < TILES)
            def _():
                at = count[c]
                count[c] = at + 1
                where[c * BLOCKS + at] = o
                rows = pl.multiple_of(at * ROWS, ROWS)
                for kb in range(KB):
                    left[c, pl.ds(rows, ROWS), kb * LANES : (kb + 1) * LANES] = piece(
                        a, b, (kb * LIVE + slot) * ROWS, ROWS
                    )

    def one_block(i, carry):
        c, r = i // SLOTS, lax.rem(i, SLOTS)

        @pl.when(live[r, c] != 0)
        def _():
            if fetches:
                pl.when(i >= EARLY)(lambda: fetch(i).wait())
            n = count[c]

            def multiply(rows, first):
                here = left[c, pl.ds(pl.multiple_of(first * ROWS, ROWS), rows), :]
                for part, ref in enumerate((mine_ref, theirs_ref)):
                    half = jnp.where(core == 0, part, 1 - part) * HALF
                    for k in range(HALF // WIDE):
                        start = pl.multiple_of(half + k * WIDE, WIDE)
                        product = jnp.dot(here, block_ref[i, :, pl.ds(start, WIDE)], preferred_element_type=f32)
                        for t in range(rows // ROWS):
                            valid = first + t < n
                            o = jnp.where(valid, where[c * BLOCKS + first + t], 0)
                            at = pl.ds(pl.multiple_of((o * SLOTS + r) * ROWS, ROWS), ROWS)
                            for m in range(WIDE // LANES):
                                term = product[t * ROWS : (t + 1) * ROWS, m * LANES : (m + 1) * LANES]
                                ref[k * (WIDE // LANES) + m, at, :] += jnp.where(valid, term, 0.0)

            low = 0
            for rows in SIZES:
                tiles = rows // ROWS
                pl.when((n > low) & ((n <= tiles) | (rows == CHUNK)))(functools.partial(multiply, rows, 0))
                low = tiles
            pl.when(n > low)(functools.partial(multiply, CHUNK, low))

        return carry

    lax.fori_loop(0, TILES * SLOTS, one_block, 0)


def compute(which, block_live, integrals, blocks, pieces):
    group = GROUPS[which]
    fetches = which == 0
    sources = {ab: (i, k * PIECE) for i, (_, held) in enumerate(pieces) for k, ab in enumerate(held)}
    total = pltpu.VMEM((RING, len(group) * SLOTS * ROWS, LANES), f32)
    more = in_vmem(blocks)
    return pl.pallas_call(
        functools.partial(compute_kernel, group, sources, fetches),
        out_shape=(total, total, pltpu.VMEM((TILES * SLOTS, ENTRY, ENTRY), bf16)),
        in_specs=[HBM, HBM] + [VMEM] * (len(pieces) + len(more)),
        out_specs=(VMEM,) * 3,
        input_output_aliases={2 + len(pieces): 2},
        scratch_shapes=[
            pltpu.VMEM((TILES, 2 * CHUNK, ENTRY), bf16),
            pltpu.VMEM((8, LANES), i32),
            pltpu.SMEM((8, LANES), i32),
            pltpu.SMEM(block_live.shape, i32),
            pltpu.SMEM((TILES,), i32),
            pltpu.SMEM((TILES * BLOCKS,), i32),
            pltpu.SemaphoreType.DMA((2,)),
            pltpu.SemaphoreType.DMA((TILES * SLOTS,)),
        ],
        compiler_params=params(8),
        cost_estimate=pl.CostEstimate(flops=1 << 32, bytes_accessed=8 << 20, transcendentals=0),
    )(*in_hbm(block_live, integrals), *[array for array, _ in pieces], *more)


def encode(value):
    top = jnp.maximum(jnp.max(jnp.abs(value), axis=0, keepdims=True), TINY)
    exponent = jnp.ceil(jnp.log(top) * (8.0 / 0.6931471805599453) + 0.01)
    inverse = jnp.exp(exponent * (-0.6931471805599453 / 8.0)) * CODE
    return jnp.round(value * inverse).astype(i32).astype(i16), exponent


def scale_of(exponent):
    return jnp.exp(exponent * (0.6931471805599453 / 8.0)) * (1.0 / CODE)


def tag_rows(sums):
    return pl.cdiv(sums, META) * META


def core_sum_kernel(mine_ref, other_ref, own_ref, *refs):
    sends, exps = refs[: RING - 1], refs[RING - 1]
    y = position()[2]
    rows = own_ref.shape[0]
    own_ref[...] = mine_ref[y] + other_ref[y]
    exps[...] = jnp.zeros_like(exps)
    for d in range(1, RING):
        q = lax.rem(y + d, RING)

        for g in range(rows // ROWS):
            at = pl.ds(g * ROWS, ROWS)
            codes, exponent = encode(mine_ref[q, at, :] + other_ref[q, at, :])
            sends[d - 1][at, :] = codes
            exps[g : g + 1, :] = exponent
        sends[d - 1][pl.ds(rows, exps.shape[0]), :] = exps[...].astype(i32).astype(i16)


def core_sum(mine, other):
    rows = mine.shape[1]
    tags = tag_rows(rows // ROWS)
    code = shape((rows + tags, LANES), i16)
    return pl.pallas_call(
        core_sum_kernel,
        out_shape=(shape((rows, LANES), f32), code, code, code),
        in_specs=[VMEM, VMEM],
        out_specs=(VMEM,) * RING,
        scratch_shapes=[pltpu.VMEM((tags, LANES), f32)],
        compiler_params=params(),
    )(mine, other)


PART = SLOTS * ROWS + META


def ring_sum_kernel(group, own_ref, a_ref, b_ref, c_ref, *refs):
    out_ref, scales, exps = refs[-3:]
    x, z = position()[:2]
    codes = (a_ref, b_ref, c_ref)
    rows, tags = own_ref.shape[0], scales.shape[1]
    for k in range(RING - 1):
        scales[k] = scale_of(codes[k][pl.ds(rows, tags), :].astype(i32).astype(f32))
    exps[...] = jnp.zeros_like(exps)
    for o, (e, d) in enumerate(group):
        to = lax.rem(x - e + RING, RING) * RING + lax.rem(z - d + RING, RING)
        for r in range(SLOTS):
            g = o * SLOTS + r
            at = pl.ds(g * ROWS, ROWS)
            total = own_ref[at, :]
            for k in range(RING - 1):
                total += codes[k][at, :].astype(i32).astype(f32) * scales[k, g : g + 1, :]
            code, exponent = encode(total)
            out_ref[to, r * ROWS : (r + 1) * ROWS, :] = code
            exps[r : r + 1, :] = exponent
        out_ref[to, SLOTS * ROWS : PART, :] = exps[...].astype(i32).astype(i16)


def ring_sum(which, own, codes, parts=None):
    more = [] if parts is None else [parts]
    return pl.pallas_call(
        functools.partial(ring_sum_kernel, GROUPS[which]),
        out_shape=shape((BLOCKS, PART, LANES), i16),
        in_specs=[VMEM] * (RING + len(more)),
        out_specs=VMEM,
        input_output_aliases={RING: 0} if more else {},
        scratch_shapes=[
            pltpu.VMEM((RING - 1, tag_rows(own.shape[0] // ROWS), LANES), f32),
            pltpu.VMEM((META, LANES), f32),
        ],
        compiler_params=params(),
    )(own, *codes, *more)


RANGES = 8
DEST = TILES * ROWS + META


def reorder_kernel(owner_ref, in_ref, out_ref, exps):
    for owner in range(BLOCKS):
        tags = in_ref[owner, SLOTS * ROWS : PART, :].astype(i32).astype(f32)
        for r in range(SLOTS):
            p = owner_ref[owner * SLOTS + r]
            v, t = p // TILES, lax.rem(p, TILES)
            rows = pl.ds(pl.multiple_of(t * ROWS, ROWS), ROWS)
            out_ref[v, rows, :] = in_ref[owner, r * ROWS : (r + 1) * ROWS, :]
            exps[pl.ds(v * META + t, 1), :] = tags[r : r + 1, :]
    for v in range(RANGES):
        out_ref[v, TILES * ROWS : DEST, :] = exps[v * META : (v + 1) * META, :].astype(i32).astype(i16)


def reorder(row_owner, parts):
    return pl.pallas_call(
        reorder_kernel,
        out_shape=shape((RANGES, DEST, LANES), i16),
        in_specs=[SMEM, VMEM],
        out_specs=VMEM,
        scratch_shapes=[pltpu.VMEM((RANGES * META, LANES), f32)],
        compiler_params=params(),
    )(pltpu.with_memory_space_constraint(row_owner, pltpu.SMEM), parts)


def finish_kernel(in_ref, out_hbm, tiles, scales, sems):
    for v in range(RANGES):
        scales[v * META : (v + 1) * META, :] = scale_of(in_ref[v, TILES * ROWS : DEST, :].astype(i32).astype(f32))
    copies = []
    for t in range(TILES):
        for v in range(RANGES):
            y, core = divmod(v, 2)
            column = core * HALF + y * LANES
            value = in_ref[v, t * ROWS : (t + 1) * ROWS, :].astype(i32).astype(f32)
            tiles[t, :, column : column + LANES] = value * scales[v * META + t : v * META + t + 1, :]
        copies.append(
            pltpu.make_async_copy(tiles.at[t], out_hbm.at[:, pl.ds(t * ENTRY, ENTRY)], sems.at[t])
        )
        copies[-1].start()
    for copy in copies:
        copy.wait()


def finish(parts):
    return pl.pallas_call(
        finish_kernel,
        out_shape=shape((ROWS, TILES * ENTRY), f32),
        in_specs=[VMEM],
        out_specs=HBM,
        scratch_shapes=[
            pltpu.VMEM((TILES, ROWS, ENTRY), f32),
            pltpu.VMEM((RANGES * META, LANES), f32),
            pltpu.SemaphoreType.DMA((TILES,)),
        ],
        compiler_params=params(),
    )(parts)


def shards(amplitudes, tile_live, integrals, block_live, row_owner):
    own = pack(tile_live, amplitudes)
    by1, by3, by2 = (shift_first(own, b) for b in (1, 3, 2))
    near = jnp.concatenate([own, by1, by3], 0)
    nears = {a: shift_second(near, a) for a in (1, 3)}
    first = [(own, [(0, 0)]), (by1, [(0, 1)]), (by3, [(0, 3)])]
    first += [(nears[a], [(a, b) for b in (0, 1, 3)]) for a in (1, 3)]
    row = jnp.concatenate([own, by1, by2, by3], 0)
    blocks, owners = fetch_blocks(block_live, integrals, row_owner, near)
    row, blocks = lax.optimization_barrier((row, blocks))
    fars = {a: shift_second(by2, a) for a in (1, 3)}
    second = [(shift_second(row, 2), [(2, b) for b in range(RING)]), (by2, [(0, 2)])]
    second += [(fars[a], [(a, 2)]) for a in (1, 3)]

    theirs0, mine0, blocks = compute(0, block_live, integrals, blocks, first)
    other0 = shift_core(theirs0)
    theirs1, mine1, _ = compute(1, block_live, integrals, blocks, second)
    other1 = shift_core(theirs1)
    own0, *sends0 = core_sum(mine0, other0)
    codes0 = [shift_y(sends0[d - 1], d) for d in range(1, RING)]
    own1, *sends1 = core_sum(mine1, other1)
    codes1 = [shift_y(sends1[d - 1], d) for d in range(1, RING)]
    parts = ring_sum(0, own0, codes0)
    parts = ring_sum(1, own1, codes1, parts)
    parts = lax.all_to_all(parts, "occ", split_axis=0, concat_axis=0, tiled=True)
    parts = reorder(owners, parts)
    parts = lax.all_to_all(parts, "vir", split_axis=0, concat_axis=0, tiled=True)
    return finish(parts)


def solution(mesh):
    return jax.shard_map(
        shards,
        mesh=mesh,
        in_specs=(
            P("occ", "vir"),
            P("occ", "vir"),
            P("occ", "vir", None, None),
            P("occ", "vir"),
            P(),
        ),
        out_specs=P("occ", "vir"),
        check_vma=False,
    )
```

```python
import functools

import jax
import jax.numpy as jnp
from jax import lax
from jax.experimental import pallas as pl
from jax.experimental.pallas import tpu as pltpu
from jax.sharding import PartitionSpec as P

RING = 4
TILES = 4
LIVE = 2
ROWS = 32
ENTRY = 1024
SLOTS = 2
BLOCKS = 16
LANES = 128
KB = ENTRY // LANES
META = 16
TAG = KB * LIVE * ROWS
PIECE = TAG + META
HALF = ENTRY // 2
CHUNK = 256
SIZES = (64, 128, CHUNK)
WIDE = 512
EARLY = 3
CODE = 32700.0
TINY = 1e-33

f32, bf16, i32, i16 = jnp.float32, jnp.bfloat16, jnp.int32, jnp.int16
VMEM = pl.BlockSpec(memory_space=pltpu.VMEM)
SMEM = pl.BlockSpec(memory_space=pltpu.SMEM)
HBM = pl.BlockSpec(memory_space=pltpu.HBM)
ANY = pl.BlockSpec(memory_space=pl.ANY)


def shape(dims, dtype):
    return jax.ShapeDtypeStruct(dims, dtype)


def position():
    occ, vir = lax.axis_index("occ"), lax.axis_index("vir")
    return occ // RING, lax.rem(occ, RING), vir // 2, lax.rem(vir, 2)


def in_hbm(*arrays):
    return [pltpu.with_memory_space_constraint(a, pltpu.HBM) for a in arrays]


def in_vmem(*arrays):
    return [pltpu.with_memory_space_constraint(a, pltpu.VMEM) for a in arrays]


def params(mib=4):
    return pltpu.CompilerParams(vmem_limit_bytes=mib * 1024 * 1024)


def pack_kernel(live_hbm, amp_hbm, out_ref, amp, live, sems):
    copies = (
        pltpu.make_async_copy(live_hbm, live, sems.at[0]),
        pltpu.make_async_copy(amp_hbm, amp, sems.at[1]),
    )
    for copy in copies:
        copy.start()
    for copy in copies:
        copy.wait()
    c0 = jnp.int32(0)
    for c in reversed(range(TILES)):
        c0 = jnp.where(live[0, c] != 0, c, c0)
    c1 = jnp.int32(TILES)
    for c in reversed(range(TILES)):
        c1 = jnp.where((live[0, c] != 0) & (c > c0), c, c1)
    for slot, c in enumerate((c0, jnp.minimum(c1, TILES - 1))):
        for kb in range(KB):
            start = pl.multiple_of(c * ENTRY + kb * LANES, LANES)
            out_ref[pl.ds((kb * LIVE + slot) * ROWS, ROWS), :] = amp[:, pl.ds(start, LANES)]
    tag = jnp.full((META, LANES), c0 * 8 + c1, i32)
    out_ref[pl.ds(TAG, META), :] = tag.astype(f32).astype(bf16)


def pack(tile_live, amplitudes):
    return pl.pallas_call(
        pack_kernel,
        out_shape=shape((PIECE, LANES), bf16),
        in_specs=[HBM, HBM],
        out_specs=VMEM,
        scratch_shapes=[
            pltpu.VMEM(amplitudes.shape, bf16),
            pltpu.SMEM(tile_live.shape, i32),
            pltpu.SemaphoreType.DMA((2,)),
        ],
        compiler_params=params(),
    )(*in_hbm(tile_live, amplitudes))


def shift(value, place):
    def index(x, z, y, core):
        return ((x % RING) * RING + z % RING) * 2 * RING + (y % RING) * 2 + core % 2

    spots = [(x, z, y, c) for x in range(RING) for z in range(RING) for y in range(RING) for c in range(2)]
    return lax.ppermute(value, ("occ", "vir"), [(index(*s), index(*place(*s))) for s in spots])


def shift_first(value, n):
    return shift(value, lambda x, z, y, c: (x, z + n, y, c) if c == 0 else (x + n, z, y, c))


def shift_second(value, n):
    return shift(value, lambda x, z, y, c: (x + n, z, y, c) if c == 0 else (x, z + n, y, c))


def shift_y(value, n):
    return shift(value, lambda x, z, y, c: (x, z, y + n, c))


def shift_core(value):
    return shift(value, lambda x, z, y, c: (x, z, y, c + 1))


def fetch_kernel(live_hbm, ints_hbm, owner_hbm, after_ref, block_ref, owner_ref, live, sem, sems):
    del after_ref
    copy = pltpu.make_async_copy(live_hbm, live, sem.at[0])
    copy.start()
    copy_owner = pltpu.make_async_copy(owner_hbm, owner_ref, sem.at[1])
    copy_owner.start()
    copy.wait()

    def fetch(i):
        return pltpu.make_async_copy(ints_hbm.at[i % SLOTS, i // SLOTS], block_ref.at[i], sems.at[i])

    for i in range(EARLY):
        pl.when(live[i % SLOTS, i // SLOTS] != 0)(functools.partial(lambda i: fetch(i).start(), i))
    for i in range(EARLY):
        pl.when(live[i % SLOTS, i // SLOTS] != 0)(functools.partial(lambda i: fetch(i).wait(), i))
    copy_owner.wait()


def fetch_blocks(block_live, integrals, row_owner, after):
    return pl.pallas_call(
        fetch_kernel,
        out_shape=(pltpu.VMEM((TILES * SLOTS, ENTRY, ENTRY), bf16), pltpu.SMEM(row_owner.shape, i32)),
        in_specs=[HBM, HBM, HBM, ANY],
        out_specs=(VMEM, SMEM),
        scratch_shapes=[
            pltpu.SMEM(block_live.shape, i32),
            pltpu.SemaphoreType.DMA((2,)),
            pltpu.SemaphoreType.DMA((EARLY,)),
        ],
        compiler_params=params(2),
        cost_estimate=pl.CostEstimate(flops=0, bytes_accessed=16 << 20, transcendentals=0),
    )(*in_hbm(block_live, integrals, row_owner), after)


NEAR = (0, 1, 3)
GROUPS = (
    [(e, d) for e in NEAR for d in NEAR],
    [(2, d) for d in range(RING)] + [(e, 2) for e in NEAR],
)


def compute_kernel(group, sources, fetches, live_hbm, ints_hbm, *refs):
    count_in = max(at for at, _ in sources.values()) + 1
    arrays = refs[:count_in]
    refs = refs[count_in + 1 :]
    theirs_ref, mine_ref, block_ref, left, table_v, table, live, count, where, sem, sems = refs
    core = position()[3]
    copy_live = pltpu.make_async_copy(live_hbm, live, sem.at[0])
    copy_live.start()

    def fetch(i):
        return pltpu.make_async_copy(ints_hbm.at[lax.rem(i, SLOTS), i // SLOTS], block_ref.at[i], sems.at[i])

    def piece(a, b, row, rows):
        at, base = sources[a, b]
        return arrays[at][pl.ds(base + row, rows), :]

    lane = lax.broadcasted_iota(i32, (8, LANES), 1)
    entries = jnp.zeros((8, LANES), i32)
    for k, (a, b) in enumerate(group):
        tag = piece(a, b, TAG, META).astype(f32)[:8].astype(i32)
        entries = jnp.where(lane == k, tag, entries)
    table_v[...] = entries
    copy_table = pltpu.make_async_copy(table_v, table, sem.at[1])
    copy_table.start()

    copy_live.wait()
    if fetches:
        for i in range(EARLY, TILES * SLOTS):
            pl.when(live[i % SLOTS, i // SLOTS] != 0)(functools.partial(lambda i: fetch(i).start(), i))
    theirs_ref[...] = jnp.zeros_like(theirs_ref)
    mine_ref[...] = jnp.zeros_like(mine_ref)
    for c in range(TILES):
        count[c] = 0
    copy_table.wait()

    for k, (a, b) in enumerate(group):
        tag = table[0, k]
        o = jnp.where(core == 0, k, group.index((b, a)))
        for slot in range(LIVE):
            c = tag // 8 if slot == 0 else lax.rem(tag, 8)

            @pl.when(c < TILES)
            def _():
                at = count[c]
                count[c] = at + 1
                where[c * BLOCKS + at] = o
                rows = pl.multiple_of(at * ROWS, ROWS)
                for kb in range(KB):
                    left[c, pl.ds(rows, ROWS), kb * LANES : (kb + 1) * LANES] = piece(
                        a, b, (kb * LIVE + slot) * ROWS, ROWS
                    )

    def one_block(i, carry):
        c, r = i // SLOTS, lax.rem(i, SLOTS)

        @pl.when(live[r, c] != 0)
        def _():
            if fetches:
                pl.when(i >= EARLY)(lambda: fetch(i).wait())
            n = count[c]

            def multiply(rows, first):
                here = left[c, pl.ds(pl.multiple_of(first * ROWS, ROWS), rows), :]
                for part, ref in enumerate((mine_ref, theirs_ref)):
                    half = jnp.where(core == 0, part, 1 - part) * HALF
                    for k in range(HALF // WIDE):
                        start = pl.multiple_of(half + k * WIDE, WIDE)
                        product = jnp.dot(here, block_ref[i, :, pl.ds(start, WIDE)], preferred_element_type=f32)
                        for t in range(rows // ROWS):
                            valid = first + t < n
                            o = jnp.where(valid, where[c * BLOCKS + first + t], 0)
                            at = pl.ds(pl.multiple_of((o * SLOTS + r) * ROWS, ROWS), ROWS)
                            for m in range(WIDE // LANES):
                                term = product[t * ROWS : (t + 1) * ROWS, m * LANES : (m + 1) * LANES]
                                ref[k * (WIDE // LANES) + m, at, :] += jnp.where(valid, term, 0.0)

            low = 0
            for rows in SIZES:
                tiles = rows // ROWS
                pl.when((n > low) & ((n <= tiles) | (rows == CHUNK)))(functools.partial(multiply, rows, 0))
                low = tiles
            pl.when(n > low)(functools.partial(multiply, CHUNK, low))

        return carry

    lax.fori_loop(0, TILES * SLOTS, one_block, 0)


def compute(which, block_live, integrals, blocks, pieces):
    group = GROUPS[which]
    fetches = which == 0
    sources = {ab: (i, k * PIECE) for i, (_, held) in enumerate(pieces) for k, ab in enumerate(held)}
    total = pltpu.VMEM((RING, len(group) * SLOTS * ROWS, LANES), f32)
    more = in_vmem(blocks)
    return pl.pallas_call(
        functools.partial(compute_kernel, group, sources, fetches),
        out_shape=(total, total, pltpu.VMEM((TILES * SLOTS, ENTRY, ENTRY), bf16)),
        in_specs=[HBM, HBM] + [VMEM] * (len(pieces) + len(more)),
        out_specs=(VMEM,) * 3,
        input_output_aliases={2 + len(pieces): 2},
        scratch_shapes=[
            pltpu.VMEM((TILES, 2 * CHUNK, ENTRY), bf16),
            pltpu.VMEM((8, LANES), i32),
            pltpu.SMEM((8, LANES), i32),
            pltpu.SMEM(block_live.shape, i32),
            pltpu.SMEM((TILES,), i32),
            pltpu.SMEM((TILES * BLOCKS,), i32),
            pltpu.SemaphoreType.DMA((2,)),
            pltpu.SemaphoreType.DMA((TILES * SLOTS,)),
        ],
        compiler_params=params(8),
        cost_estimate=pl.CostEstimate(flops=1 << 32, bytes_accessed=8 << 20, transcendentals=0),
    )(*in_hbm(block_live, integrals), *[array for array, _ in pieces], *more)


def encode(value):
    top = jnp.maximum(jnp.max(jnp.abs(value), axis=0, keepdims=True), TINY)
    exponent = jnp.ceil(jnp.log(top) * (8.0 / 0.6931471805599453) + 0.01)
    inverse = jnp.exp(exponent * (-0.6931471805599453 / 8.0)) * CODE
    return jnp.round(value * inverse).astype(i32).astype(i16), exponent


def scale_of(exponent):
    return jnp.exp(exponent * (0.6931471805599453 / 8.0)) * (1.0 / CODE)


def tag_rows(sums):
    return pl.cdiv(sums, META) * META


def core_sum_kernel(mine_ref, other_ref, own_ref, *refs):
    sends, exps = refs[: RING - 1], refs[RING - 1]
    y = position()[2]
    rows = own_ref.shape[0]
    own_ref[...] = mine_ref[y] + other_ref[y]
    exps[...] = jnp.zeros_like(exps)
    for d in range(1, RING):
        q = lax.rem(y + d, RING)

        for g in range(rows // ROWS):
            at = pl.ds(g * ROWS, ROWS)
            codes, exponent = encode(mine_ref[q, at, :] + other_ref[q, at, :])
            sends[d - 1][at, :] = codes
            exps[g : g + 1, :] = exponent
        sends[d - 1][pl.ds(rows, exps.shape[0]), :] = exps[...].astype(i32).astype(i16)


def core_sum(mine, other):
    rows = mine.shape[1]
    tags = tag_rows(rows // ROWS)
    code = shape((rows + tags, LANES), i16)
    return pl.pallas_call(
        core_sum_kernel,
        out_shape=(shape((rows, LANES), f32), code, code, code),
        in_specs=[VMEM, VMEM],
        out_specs=(VMEM,) * RING,
        scratch_shapes=[pltpu.VMEM((tags, LANES), f32)],
        compiler_params=params(),
    )(mine, other)


PART = SLOTS * ROWS + META


def ring_sum_kernel(group, own_ref, a_ref, b_ref, c_ref, *refs):
    out_ref, scales, exps = refs[-3:]
    x, z = position()[:2]
    codes = (a_ref, b_ref, c_ref)
    rows, tags = own_ref.shape[0], scales.shape[1]
    for k in range(RING - 1):
        scales[k] = scale_of(codes[k][pl.ds(rows, tags), :].astype(i32).astype(f32))
    exps[...] = jnp.zeros_like(exps)
    for o, (e, d) in enumerate(group):
        to = lax.rem(x - e + RING, RING) * RING + lax.rem(z - d + RING, RING)
        for r in range(SLOTS):
            g = o * SLOTS + r
            at = pl.ds(g * ROWS, ROWS)
            total = own_ref[at, :]
            for k in range(RING - 1):
                total += codes[k][at, :].astype(i32).astype(f32) * scales[k, g : g + 1, :]
            code, exponent = encode(total)
            out_ref[to, r * ROWS : (r + 1) * ROWS, :] = code
            exps[r : r + 1, :] = exponent
        out_ref[to, SLOTS * ROWS : PART, :] = exps[...].astype(i32).astype(i16)


def ring_sum(which, own, codes, parts=None):
    more = [] if parts is None else [parts]
    return pl.pallas_call(
        functools.partial(ring_sum_kernel, GROUPS[which]),
        out_shape=shape((BLOCKS, PART, LANES), i16),
        in_specs=[VMEM] * (RING + len(more)),
        out_specs=VMEM,
        input_output_aliases={RING: 0} if more else {},
        scratch_shapes=[
            pltpu.VMEM((RING - 1, tag_rows(own.shape[0] // ROWS), LANES), f32),
            pltpu.VMEM((META, LANES), f32),
        ],
        compiler_params=params(),
    )(own, *codes, *more)


RANGES = 8
DEST = TILES * ROWS + META


def reorder_kernel(owner_ref, in_ref, out_ref, exps):
    for owner in range(BLOCKS):
        tags = in_ref[owner, SLOTS * ROWS : PART, :].astype(i32).astype(f32)
        for r in range(SLOTS):
            p = owner_ref[owner * SLOTS + r]
            v, t = p // TILES, lax.rem(p, TILES)
            rows = pl.ds(pl.multiple_of(t * ROWS, ROWS), ROWS)
            out_ref[v, rows, :] = in_ref[owner, r * ROWS : (r + 1) * ROWS, :]
            exps[pl.ds(v * META + t, 1), :] = tags[r : r + 1, :]
    for v in range(RANGES):
        out_ref[v, TILES * ROWS : DEST, :] = exps[v * META : (v + 1) * META, :].astype(i32).astype(i16)


def reorder(row_owner, parts):
    return pl.pallas_call(
        reorder_kernel,
        out_shape=shape((RANGES, DEST, LANES), i16),
        in_specs=[SMEM, VMEM],
        out_specs=VMEM,
        scratch_shapes=[pltpu.VMEM((RANGES * META, LANES), f32)],
        compiler_params=params(),
    )(pltpu.with_memory_space_constraint(row_owner, pltpu.SMEM), parts)


def finish_kernel(in_ref, out_hbm, tiles, scales, sems):
    for v in range(RANGES):
        scales[v * META : (v + 1) * META, :] = scale_of(in_ref[v, TILES * ROWS : DEST, :].astype(i32).astype(f32))
    copies = []
    for t in range(TILES):
        for v in range(RANGES):
            y, core = divmod(v, 2)
            column = core * HALF + y * LANES
            value = in_ref[v, t * ROWS : (t + 1) * ROWS, :].astype(i32).astype(f32)
            tiles[t, :, column : column + LANES] = value * scales[v * META + t : v * META + t + 1, :]
        copies.append(
            pltpu.make_async_copy(tiles.at[t], out_hbm.at[:, pl.ds(t * ENTRY, ENTRY)], sems.at[t])
        )
        copies[-1].start()
    for copy in copies:
        copy.wait()


def finish(parts):
    return pl.pallas_call(
        finish_kernel,
        out_shape=shape((ROWS, TILES * ENTRY), f32),
        in_specs=[VMEM],
        out_specs=HBM,
        scratch_shapes=[
            pltpu.VMEM((TILES, ROWS, ENTRY), f32),
            pltpu.VMEM((RANGES * META, LANES), f32),
            pltpu.SemaphoreType.DMA((TILES,)),
        ],
        compiler_params=params(),
    )(parts)


def shards(amplitudes, tile_live, integrals, block_live, row_owner):
    own = pack(tile_live, amplitudes)
    by1, by3, by2 = (shift_first(own, b) for b in (1, 3, 2))
    near = jnp.concatenate([own, by1, by3], 0)
    nears = {a: shift_second(near, a) for a in (1, 3)}
    first = [(own, [(0, 0)]), (by1, [(0, 1)]), (by3, [(0, 3)])]
    first += [(nears[a], [(a, b) for b in (0, 1, 3)]) for a in (1, 3)]
    row = jnp.concatenate([own, by1, by2, by3], 0)
    blocks, owners = fetch_blocks(block_live, integrals, row_owner, near)
    row, blocks = lax.optimization_barrier((row, blocks))
    fars = {a: shift_second(by2, a) for a in (1, 3)}
    second = [(shift_second(row, 2), [(2, b) for b in range(RING)]), (by2, [(0, 2)])]
    second += [(fars[a], [(a, 2)]) for a in (1, 3)]

    theirs0, mine0, blocks = compute(0, block_live, integrals, blocks, first)
    other0 = shift_core(theirs0)
    theirs1, mine1, _ = compute(1, block_live, integrals, blocks, second)
    other1 = shift_core(theirs1)
    own0, *sends0 = core_sum(mine0, other0)
    codes0 = [shift_y(sends0[d - 1], d) for d in range(1, RING)]
    own1, *sends1 = core_sum(mine1, other1)
    codes1 = [shift_y(sends1[d - 1], d) for d in range(1, RING)]
    parts = ring_sum(0, own0, codes0)
    parts = ring_sum(1, own1, codes1, parts)
    parts = lax.all_to_all(parts, "occ", split_axis=0, concat_axis=0, tiled=True)
    parts = reorder(owners, parts)
    parts = lax.all_to_all(parts, "vir", split_axis=0, concat_axis=0, tiled=True)
    return finish(parts)


def solution(mesh):
    return jax.shard_map(
        shards,
        mesh=mesh,
        in_specs=(
            P("occ", "vir"),
            P("occ", "vir"),
            P("occ", "vir", None, None),
            P("occ", "vir"),
            P(),
        ),
        out_specs=P("occ", "vir"),
        check_vma=False,
    )
```

```python
import functools

import jax
import jax.numpy as jnp
from jax import lax
from jax.experimental import pallas as pl
from jax.experimental.pallas import tpu as pltpu
from jax.sharding import PartitionSpec as P

RING = 4
TILES = 4
LIVE = 2
ROWS = 32
ENTRY = 1024
SLOTS = 2
BLOCKS = 16
LANES = 128
KB = ENTRY // LANES
META = 16
TAG = KB * LIVE * ROWS
PIECE = TAG + META
HALF = ENTRY // 2
CHUNK = 256
SIZES = (64, 128, CHUNK)
WIDE = 512
EARLY = 3
CODE = 32700.0
TINY = 1e-33

f32, bf16, i32, i16 = jnp.float32, jnp.bfloat16, jnp.int32, jnp.int16
VMEM = pl.BlockSpec(memory_space=pltpu.VMEM)
SMEM = pl.BlockSpec(memory_space=pltpu.SMEM)
HBM = pl.BlockSpec(memory_space=pltpu.HBM)
ANY = pl.BlockSpec(memory_space=pl.ANY)


def shape(dims, dtype):
    return jax.ShapeDtypeStruct(dims, dtype)


def position():
    occ, vir = lax.axis_index("occ"), lax.axis_index("vir")
    return occ // RING, lax.rem(occ, RING), vir // 2, lax.rem(vir, 2)


def in_hbm(*arrays):
    return [pltpu.with_memory_space_constraint(a, pltpu.HBM) for a in arrays]


def in_smem(array):
    return pltpu.with_memory_space_constraint(array, pltpu.SMEM)


def in_vmem(*arrays):
    return [pltpu.with_memory_space_constraint(a, pltpu.VMEM) for a in arrays]


def params(mib=4):
    return pltpu.CompilerParams(vmem_limit_bytes=mib * 1024 * 1024)


def pack_kernel(live_hbm, amp_hbm, out_ref, amp, live, sems):
    copies = (
        pltpu.make_async_copy(live_hbm, live, sems.at[0]),
        pltpu.make_async_copy(amp_hbm, amp, sems.at[1]),
    )
    for copy in copies:
        copy.start()
    for copy in copies:
        copy.wait()
    c0 = jnp.int32(0)
    for c in reversed(range(TILES)):
        c0 = jnp.where(live[0, c] != 0, c, c0)
    c1 = jnp.int32(TILES)
    for c in reversed(range(TILES)):
        c1 = jnp.where((live[0, c] != 0) & (c > c0), c, c1)
    for slot, c in enumerate((c0, jnp.minimum(c1, TILES - 1))):
        for kb in range(KB):
            start = pl.multiple_of(c * ENTRY + kb * LANES, LANES)
            out_ref[pl.ds((kb * LIVE + slot) * ROWS, ROWS), :] = amp[:, pl.ds(start, LANES)]
    tag = jnp.full((META, LANES), c0 * 8 + c1, i32)
    out_ref[pl.ds(TAG, META), :] = tag.astype(f32).astype(bf16)


def pack(tile_live, amplitudes):
    return pl.pallas_call(
        pack_kernel,
        out_shape=shape((PIECE, LANES), bf16),
        in_specs=[HBM, HBM],
        out_specs=VMEM,
        scratch_shapes=[
            pltpu.VMEM(amplitudes.shape, bf16),
            pltpu.SMEM(tile_live.shape, i32),
            pltpu.SemaphoreType.DMA((2,)),
        ],
        compiler_params=params(),
    )(*in_hbm(tile_live, amplitudes))


def shift(value, place):
    def index(x, z, y, core):
        return ((x % RING) * RING + z % RING) * 2 * RING + (y % RING) * 2 + core % 2

    spots = [(x, z, y, c) for x in range(RING) for z in range(RING) for y in range(RING) for c in range(2)]
    return lax.ppermute(value, ("occ", "vir"), [(index(*s), index(*place(*s))) for s in spots])


def shift_first(value, n):
    return shift(value, lambda x, z, y, c: (x, z + n, y, c) if c == 0 else (x + n, z, y, c))


def shift_second(value, n):
    return shift(value, lambda x, z, y, c: (x + n, z, y, c) if c == 0 else (x, z + n, y, c))


def shift_y(value, n):
    return shift(value, lambda x, z, y, c: (x, z, y + n, c))


def shift_core(value):
    return shift(value, lambda x, z, y, c: (x, z, y, c + 1))


def fetch_kernel(live_hbm, ints_hbm, owner_hbm, after_ref, block_ref, owner_ref, live, sem, sems):
    del after_ref
    copy = pltpu.make_async_copy(live_hbm, live, sem.at[0])
    copy.start()
    copy_owner = pltpu.make_async_copy(owner_hbm, owner_ref, sem.at[1])
    copy_owner.start()
    copy.wait()

    def fetch(i):
        return pltpu.make_async_copy(ints_hbm.at[i % SLOTS, i // SLOTS], block_ref.at[i], sems.at[i])

    for i in range(EARLY):
        pl.when(live[i % SLOTS, i // SLOTS] != 0)(functools.partial(lambda i: fetch(i).start(), i))
    for i in range(EARLY):
        pl.when(live[i % SLOTS, i // SLOTS] != 0)(functools.partial(lambda i: fetch(i).wait(), i))
    copy_owner.wait()


def fetch_blocks(block_live, integrals, row_owner, after):
    return pl.pallas_call(
        fetch_kernel,
        out_shape=(pltpu.VMEM((TILES * SLOTS, ENTRY, ENTRY), bf16), pltpu.SMEM(row_owner.shape, i32), pltpu.SMEM(block_live.shape, i32)),
        in_specs=[HBM, HBM, HBM, ANY],
        out_specs=(VMEM, SMEM, SMEM),
        scratch_shapes=[
            pltpu.SemaphoreType.DMA((2,)),
            pltpu.SemaphoreType.DMA((EARLY,)),
        ],
        compiler_params=params(2),
        cost_estimate=pl.CostEstimate(flops=0, bytes_accessed=16 << 20, transcendentals=0),
    )(*in_hbm(block_live, integrals, row_owner), after)


NEAR = (0, 1, 3)
GROUPS = (
    [(e, d) for e in NEAR for d in NEAR],
    [(2, d) for d in range(RING)] + [(e, 2) for e in NEAR],
)


def compute_kernel(group, sources, fetches, live, ints_hbm, *refs):
    count_in = max(at for at, _ in sources.values()) + 1
    arrays = refs[:count_in]
    refs = refs[count_in + 1 :]
    theirs_ref, mine_ref, block_ref, left, table_v, table, count, where, sem, sems = refs
    core = position()[3]

    def fetch(i):
        return pltpu.make_async_copy(ints_hbm.at[lax.rem(i, SLOTS), i // SLOTS], block_ref.at[i], sems.at[i])

    def piece(a, b, row, rows):
        at, base = sources[a, b]
        return arrays[at][pl.ds(base + row, rows), :]

    if fetches:
        for i in range(EARLY, TILES * SLOTS):
            pl.when(live[i % SLOTS, i // SLOTS] != 0)(functools.partial(lambda i: fetch(i).start(), i))

    lane = lax.broadcasted_iota(i32, (8, LANES), 1)
    entries = jnp.zeros((8, LANES), i32)
    for k, (a, b) in enumerate(group):
        tag = piece(a, b, TAG, META).astype(f32)[:8].astype(i32)
        entries = jnp.where(lane == k, tag, entries)
    table_v[...] = entries
    copy_table = pltpu.make_async_copy(table_v, table, sem)
    copy_table.start()

    theirs_ref[...] = jnp.zeros_like(theirs_ref)
    mine_ref[...] = jnp.zeros_like(mine_ref)
    for c in range(TILES):
        count[c] = 0
    copy_table.wait()

    for k, (a, b) in enumerate(group):
        tag = table[0, k]
        o = jnp.where(core == 0, k, group.index((b, a)))
        for slot in range(LIVE):
            c = tag // 8 if slot == 0 else lax.rem(tag, 8)

            @pl.when(c < TILES)
            def _():
                at = count[c]
                count[c] = at + 1
                where[c * BLOCKS + at] = o
                rows = pl.multiple_of(at * ROWS, ROWS)
                for kb in range(KB):
                    left[c, pl.ds(rows, ROWS), kb * LANES : (kb + 1) * LANES] = piece(
                        a, b, (kb * LIVE + slot) * ROWS, ROWS
                    )

    def one_block(i, carry):
        c, r = i // SLOTS, lax.rem(i, SLOTS)

        @pl.when(live[r, c] != 0)
        def _():
            if fetches:
                pl.when(i >= EARLY)(lambda: fetch(i).wait())
            n = count[c]

            def multiply(rows, first):
                here = left[c, pl.ds(pl.multiple_of(first * ROWS, ROWS), rows), :]
                for part, ref in enumerate((mine_ref, theirs_ref)):
                    half = jnp.where(core == 0, part, 1 - part) * HALF
                    for k in range(HALF // WIDE):
                        start = pl.multiple_of(half + k * WIDE, WIDE)
                        product = jnp.dot(here, block_ref[i, :, pl.ds(start, WIDE)], preferred_element_type=f32)
                        for t in range(rows // ROWS):
                            valid = first + t < n
                            o = jnp.where(valid, where[c * BLOCKS + first + t], 0)
                            at = pl.ds(pl.multiple_of((o * SLOTS + r) * ROWS, ROWS), ROWS)
                            for m in range(WIDE // LANES):
                                term = product[t * ROWS : (t + 1) * ROWS, m * LANES : (m + 1) * LANES]
                                ref[k * (WIDE // LANES) + m, at, :] += jnp.where(valid, term, 0.0)

            low = 0
            for rows in SIZES:
                tiles = rows // ROWS
                pl.when((n > low) & ((n <= tiles) | (rows == CHUNK)))(functools.partial(multiply, rows, 0))
                low = tiles
            pl.when(n > low)(functools.partial(multiply, CHUNK, low))

        return carry

    lax.fori_loop(0, TILES * SLOTS, one_block, 0)


def compute(which, flags, integrals, blocks, pieces):
    group = GROUPS[which]
    fetches = which == 0
    sources = {ab: (i, k * PIECE) for i, (_, held) in enumerate(pieces) for k, ab in enumerate(held)}
    total = pltpu.VMEM((RING, len(group) * SLOTS * ROWS, LANES), f32)
    more = in_vmem(blocks)
    return pl.pallas_call(
        functools.partial(compute_kernel, group, sources, fetches),
        out_shape=(total, total, pltpu.VMEM((TILES * SLOTS, ENTRY, ENTRY), bf16)),
        in_specs=[SMEM, HBM] + [VMEM] * (len(pieces) + len(more)),
        out_specs=(VMEM,) * 3,
        input_output_aliases={2 + len(pieces): 2},
        scratch_shapes=[
            pltpu.VMEM((TILES, 2 * CHUNK, ENTRY), bf16),
            pltpu.VMEM((8, LANES), i32),
            pltpu.SMEM((8, LANES), i32),
            pltpu.SMEM((TILES,), i32),
            pltpu.SMEM((TILES * BLOCKS,), i32),
            pltpu.SemaphoreType.DMA,
            pltpu.SemaphoreType.DMA((TILES * SLOTS,)),
        ],
        compiler_params=params(8),
        cost_estimate=pl.CostEstimate(flops=1 << 32, bytes_accessed=8 << 20, transcendentals=0),
    )(in_smem(flags), *in_hbm(integrals), *[array for array, _ in pieces], *more)


def encode(value):
    top = jnp.maximum(jnp.max(jnp.abs(value), axis=0, keepdims=True), TINY)
    exponent = jnp.ceil(jnp.log(top) * (8.0 / 0.6931471805599453) + 0.01)
    inverse = jnp.exp(exponent * (-0.6931471805599453 / 8.0)) * CODE
    return jnp.round(value * inverse).astype(i32).astype(i16), exponent


def scale_of(exponent):
    return jnp.exp(exponent * (0.6931471805599453 / 8.0)) * (1.0 / CODE)


def tag_rows(sums):
    return pl.cdiv(sums, META) * META


def core_sum_kernel(mine_ref, other_ref, own_ref, *refs):
    sends, exps = refs[: RING - 1], refs[RING - 1]
    y = position()[2]
    rows = own_ref.shape[0]
    own_ref[...] = mine_ref[y] + other_ref[y]
    exps[...] = jnp.zeros_like(exps)
    for d in range(1, RING):
        q = lax.rem(y + d, RING)

        for g in range(rows // ROWS):
            at = pl.ds(g * ROWS, ROWS)
            codes, exponent = encode(mine_ref[q, at, :] + other_ref[q, at, :])
            sends[d - 1][at, :] = codes
            exps[g : g + 1, :] = exponent
        sends[d - 1][pl.ds(rows, exps.shape[0]), :] = exps[...].astype(i32).astype(i16)


def core_sum(mine, other):
    rows = mine.shape[1]
    tags = tag_rows(rows // ROWS)
    code = shape((rows + tags, LANES), i16)
    return pl.pallas_call(
        core_sum_kernel,
        out_shape=(shape((rows, LANES), f32), code, code, code),
        in_specs=[VMEM, VMEM],
        out_specs=(VMEM,) * RING,
        scratch_shapes=[pltpu.VMEM((tags, LANES), f32)],
        compiler_params=params(),
    )(mine, other)


PART = SLOTS * ROWS + META


def ring_sum_kernel(group, own_ref, a_ref, b_ref, c_ref, *refs):
    out_ref, scales, exps = refs[-3:]
    x, z = position()[:2]
    codes = (a_ref, b_ref, c_ref)
    rows, tags = own_ref.shape[0], scales.shape[1]
    for k in range(RING - 1):
        scales[k] = scale_of(codes[k][pl.ds(rows, tags), :].astype(i32).astype(f32))
    exps[...] = jnp.zeros_like(exps)
    for o, (e, d) in enumerate(group):
        to = lax.rem(x - e + RING, RING) * RING + lax.rem(z - d + RING, RING)
        for r in range(SLOTS):
            g = o * SLOTS + r
            at = pl.ds(g * ROWS, ROWS)
            total = own_ref[at, :]
            for k in range(RING - 1):
                total += codes[k][at, :].astype(i32).astype(f32) * scales[k, g : g + 1, :]
            code, exponent = encode(total)
            out_ref[to, r * ROWS : (r + 1) * ROWS, :] = code
            exps[r : r + 1, :] = exponent
        out_ref[to, SLOTS * ROWS : PART, :] = exps[...].astype(i32).astype(i16)


def ring_sum(which, own, codes, parts=None):
    more = [] if parts is None else [parts]
    return pl.pallas_call(
        functools.partial(ring_sum_kernel, GROUPS[which]),
        out_shape=shape((BLOCKS, PART, LANES), i16),
        in_specs=[VMEM] * (RING + len(more)),
        out_specs=VMEM,
        input_output_aliases={RING: 0} if more else {},
        scratch_shapes=[
            pltpu.VMEM((RING - 1, tag_rows(own.shape[0] // ROWS), LANES), f32),
            pltpu.VMEM((META, LANES), f32),
        ],
        compiler_params=params(),
    )(own, *codes, *more)


RANGES = 8
DEST = TILES * ROWS + META


def reorder_kernel(owner_ref, in_ref, out_ref, exps):
    for owner in range(BLOCKS):
        tags = in_ref[owner, SLOTS * ROWS : PART, :].astype(i32).astype(f32)
        for r in range(SLOTS):
            p = owner_ref[owner * SLOTS + r]
            v, t = p // TILES, lax.rem(p, TILES)
            rows = pl.ds(pl.multiple_of(t * ROWS, ROWS), ROWS)
            out_ref[v, rows, :] = in_ref[owner, r * ROWS : (r + 1) * ROWS, :]
            exps[pl.ds(v * META + t, 1), :] = tags[r : r + 1, :]
    for v in range(RANGES):
        out_ref[v, TILES * ROWS : DEST, :] = exps[v * META : (v + 1) * META, :].astype(i32).astype(i16)


def reorder(row_owner, parts):
    return pl.pallas_call(
        reorder_kernel,
        out_shape=shape((RANGES, DEST, LANES), i16),
        in_specs=[SMEM, VMEM],
        out_specs=VMEM,
        scratch_shapes=[pltpu.VMEM((RANGES * META, LANES), f32)],
        compiler_params=params(),
    )(in_smem(row_owner), parts)


def finish_kernel(in_ref, out_hbm, tiles, scales, sems):
    for v in range(RANGES):
        scales[v * META : (v + 1) * META, :] = scale_of(in_ref[v, TILES * ROWS : DEST, :].astype(i32).astype(f32))
    copies = []
    for t in range(TILES):
        for v in range(RANGES):
            y, core = divmod(v, 2)
            column = core * HALF + y * LANES
            value = in_ref[v, t * ROWS : (t + 1) * ROWS, :].astype(i32).astype(f32)
            tiles[t, :, column : column + LANES] = value * scales[v * META + t : v * META + t + 1, :]
        copies.append(
            pltpu.make_async_copy(tiles.at[t], out_hbm.at[:, pl.ds(t * ENTRY, ENTRY)], sems.at[t])
        )
        copies[-1].start()
    for copy in copies:
        copy.wait()


def finish(parts):
    return pl.pallas_call(
        finish_kernel,
        out_shape=shape((ROWS, TILES * ENTRY), f32),
        in_specs=[VMEM],
        out_specs=HBM,
        scratch_shapes=[
            pltpu.VMEM((TILES, ROWS, ENTRY), f32),
            pltpu.VMEM((RANGES * META, LANES), f32),
            pltpu.SemaphoreType.DMA((TILES,)),
        ],
        compiler_params=params(),
    )(parts)


def shards(amplitudes, tile_live, integrals, block_live, row_owner):
    own = pack(tile_live, amplitudes)
    by1, by3, by2 = (shift_first(own, b) for b in (1, 3, 2))
    near = jnp.concatenate([own, by1, by3], 0)
    nears = {a: shift_second(near, a) for a in (1, 3)}
    first = [(own, [(0, 0)]), (by1, [(0, 1)]), (by3, [(0, 3)])]
    first += [(nears[a], [(a, b) for b in (0, 1, 3)]) for a in (1, 3)]
    row = jnp.concatenate([own, by1, by2, by3], 0)
    blocks, owners, flags = fetch_blocks(block_live, integrals, row_owner, near)
    row, blocks = lax.optimization_barrier((row, blocks))
    fars = {a: shift_second(by2, a) for a in (1, 3)}
    second = [(shift_second(row, 2), [(2, b) for b in range(RING)]), (by2, [(0, 2)])]
    second += [(fars[a], [(a, 2)]) for a in (1, 3)]

    theirs0, mine0, blocks = compute(0, flags, integrals, blocks, first)
    other0 = shift_core(theirs0)
    theirs1, mine1, _ = compute(1, flags, integrals, blocks, second)
    other1 = shift_core(theirs1)
    own0, *sends0 = core_sum(mine0, other0)
    codes0 = [shift_y(sends0[d - 1], d) for d in range(1, RING)]
    own1, *sends1 = core_sum(mine1, other1)
    codes1 = [shift_y(sends1[d - 1], d) for d in range(1, RING)]
    parts = ring_sum(0, own0, codes0)
    parts = ring_sum(1, own1, codes1, parts)
    parts = lax.all_to_all(parts, "occ", split_axis=0, concat_axis=0, tiled=True)
    parts = reorder(owners, parts)
    parts = lax.all_to_all(parts, "vir", split_axis=0, concat_axis=0, tiled=True)
    return finish(parts)


def solution(mesh):
    return jax.shard_map(
        shards,
        mesh=mesh,
        in_specs=(
            P("occ", "vir"),
            P("occ", "vir"),
            P("occ", "vir", None, None),
            P("occ", "vir"),
            P(),
        ),
        out_specs=P("occ", "vir"),
        check_vma=False,
    )
```
